32 devices in a mesh: src: 2 (over x), rcv: 4 (over z), sp: 4 (over y, core).
Axes of the slice: x: 2, y: 2, z: 4, core: 2. Of those that a mesh axis runs over, the one named last changes fastest.
Arguments:
- shot_traces: float32 [32, 64, 1024], P('sp', 'src', 'rcv'), may hold values from -0.06 to 0.06
- surface_receiver_traces: float32 [32, 128, 1024], P('sp', 'rcv', 'src'), may hold values from -0.06 to 0.06
- obliquity: float32 [32], P('sp'), may hold values from 0.3 to 1
- lowest_receiver_index: int32 [32], P('sp'), may hold values from 0 to 31
- hi_index: int32 [32], P('sp'), may hold values from 96 to 127
Outputs:
- multiples: float32 [512, 2, 64, 128], P('sp', None, 'src', 'rcv')
The draws below stay inside these ranges and needn't reach their ends.
All inputs are finite; a program needn't handle non-finite values.
Results may differ from the reference program's by a relative error of at most 0.000098.
Values sent between devices are 32-bit elements; how exact they have to be, the bound alone decides.
No kernel may reach another device: no remote copies, remote signals or barrier semaphores. Data moves between devices by JAX's collectives and lax.ppermute only.
A program may use at most 128 MiB of HBM per device.

```python
import math
import jax
import jax.numpy as jnp
from jax import lax

NT = 1024
NF = 512
S = 64
R = 128
X = 32
RAMP = 16


def place_ends(result, rng, low, largest):
    longest = result.shape.index(max(result.shape))
    spots = []
    for shift in (0, 1):
        where = [jax.random.randint(jax.random.fold_in(rng, axis), (), 0, length) for axis, length in enumerate(result.shape)]
        where[longest] = (where[longest] + shift) % result.shape[longest]
        spots.append(tuple(where))
    return result.at[spots[0]].set(low).at[spots[1]].set(largest)


def shard_levels(own_key, extent, pieces, smallest, high):
    gain = 1.0
    for axis_at, blocks in pieces:
        steps = jax.random.uniform(jax.random.fold_in(jax.random.fold_in(own_key, 6), axis_at), (blocks,), jnp.float32, smallest / len(pieces), high / len(pieces))
        gain = gain * jnp.repeat(jnp.exp(steps), extent[axis_at] // blocks).reshape((-1,) + (1,) * (len(extent) - 1 - axis_at))
    return gain


def bell_draw(key, extent, spread, most, pieces=(), held_as=jnp.bfloat16):
    result = spread * jax.random.normal(key, extent, jnp.float32)
    if pieces:
        result = result * shard_levels(key, extent, pieces, -0.22, 0.18)
    return jnp.clip(result, -most, most).astype(held_as)


def setup_inputs(seed: int = 0) -> dict:
    seeds = jax.random.split(jax.random.key(seed), 6)
    shot_traces = bell_draw(seeds[0], (X, S, NT), 0.01, 0.06, ((0, 4), (1, 2), (2, 4)), jnp.float32)
    surface_receiver_traces = bell_draw(seeds[1], (X, R, NT), 0.01, 0.06, ((0, 4), (1, 4), (2, 2)), jnp.float32)
    obliquity = jnp.clip(jnp.exp(math.log(1.0) - 1.2039728 * jax.random.uniform(seeds[2], (X,), jnp.float32) ** shard_levels(seeds[2], (X,), ((0, 4),), -0.2, 0.2)), 0.3, 1.0)
    lowest_receiver_index = place_ends(jax.random.randint(seeds[3], (X,), 0, R // 4), jax.random.fold_in(seeds[3], 1), 0, (R // 4) - 1).astype(jnp.int32)
    hi_index = place_ends(jax.random.randint(seeds[4], (X,), 3 * R // 4, R), jax.random.fold_in(seeds[4], 1), 3 * R // 4, R - 1).astype(jnp.int32)
    return {"shot_traces": shot_traces, "surface_receiver_traces": surface_receiver_traces, "obliquity": obliquity, "lowest_receiver_index": lowest_receiver_index, "hi_index": hi_index}


def fourier_table(samples, bins):
    times = jnp.arange(samples, dtype=jnp.int32)[:, None]
    freqs = jnp.arange(bins, dtype=jnp.int32)[None, :]
    phases = ((times * freqs) % samples).astype(jnp.float32) * (2.0 * math.pi / samples)
    return jnp.concatenate([jnp.cos(phases), -jnp.sin(phases)], axis=1)


def receiver_taper(obliquity, lowest_receiver_index, hi_index, first_receiver, receivers, ramp_width):
    columns = first_receiver + jnp.arange(receivers, dtype=jnp.int32)
    rising = jnp.clip((columns[None, :] - lowest_receiver_index[:, None] + 1).astype(jnp.float32) / ramp_width, 0.0, 1.0)
    falling = jnp.clip((hi_index[:, None] - columns[None, :] + 1).astype(jnp.float32) / ramp_width, 0.0, 1.0)
    return obliquity[:, None] * rising * falling


def multiply_bands(source_frequency_spectrum, receiver_frequency_spectrum):
    maximum_precision = lax.Precision.HIGHEST
    real_component = jnp.einsum("bio,bjo->oij", source_frequency_spectrum[:, :, 0], receiver_frequency_spectrum[:, :, 0], precision=maximum_precision) - jnp.einsum("bio,bjo->oij", source_frequency_spectrum[:, :, 1], receiver_frequency_spectrum[:, :, 1], precision=maximum_precision)
    imaginary_component = jnp.einsum("bio,bjo->oij", source_frequency_spectrum[:, :, 0], receiver_frequency_spectrum[:, :, 1], precision=maximum_precision) + jnp.einsum("bio,bjo->oij", source_frequency_spectrum[:, :, 1], receiver_frequency_spectrum[:, :, 0], precision=maximum_precision)
    return jnp.stack([real_component, imaginary_component], axis=1)


def reference(shot_traces, surface_receiver_traces, obliquity, lowest_receiver_index, hi_index):
    maximum_precision = lax.Precision.HIGHEST
    fourier = fourier_table(NT, NF)
    source_frequency_spectrum = jnp.dot(shot_traces.reshape(X * S, NT), fourier, precision=maximum_precision).reshape(X, S, 2, NF)
    receiver_frequency_spectrum = jnp.dot(surface_receiver_traces.reshape(X * R, NT), fourier, precision=maximum_precision).reshape(X, R, 2, NF)
    aperture_weights = receiver_taper(obliquity, lowest_receiver_index, hi_index, 0, R, RAMP)
    receiver_frequency_spectrum = receiver_frequency_spectrum * aperture_weights[:, :, None, None]
    return multiply_bands(source_frequency_spectrum, receiver_frequency_spectrum)
```

```python
import math

import jax
import jax.numpy as jnp
import ml_dtypes
import numpy as np
from jax import lax
from jax.experimental import pallas as pl
from jax.experimental.pallas import tpu as pltpu
from jax.sharding import PartitionSpec as P

NF = 512
VMEM = pl.BlockSpec(memory_space=pltpu.VMEM)
SMEM = pl.BlockSpec(memory_space=pltpu.SMEM)


def split_table(samples, bins, parts):
    times = np.arange(samples, dtype=np.int64)[:, None]
    freqs = np.arange(bins, dtype=np.int64)[None, :]
    phases = (times * freqs % samples) * (2.0 * math.pi / samples)
    table = np.stack([np.cos(phases), -np.sin(phases)]).astype(np.float32)
    table = table.reshape(2, samples, parts, bins // parts).transpose(2, 1, 0, 3)
    table = table.reshape(parts, samples, 2 * (bins // parts))
    high = table.astype(ml_dtypes.bfloat16)
    low = (table - high.astype(np.float32)).astype(ml_dtypes.bfloat16)
    return high, low


def transform_kernel(pieces, parts, ramp, *refs):
    where_ref, refs = refs[0], refs[1:]
    if ramp:
        (obliquity_ref, lowest_ref, highest_ref), refs = refs[:3], refs[3:]
    piece_refs, refs = refs[:pieces], refs[pieces:]
    (high_ref, low_ref), refs = refs[:2], refs[2:]
    out_refs, (x_high, x_low) = refs[:parts], refs[parts:]
    me_time, me_sp, first_point = where_ref[0], where_ref[1], where_ref[2]
    points, rows, width = piece_refs[0].shape
    bins = out_refs[0].shape[-1]
    for j in range(pieces):
        x = piece_refs[j][...].reshape(points * rows, width)
        high = x.astype(jnp.bfloat16)
        low = (x - high.astype(jnp.float32)).astype(jnp.bfloat16)
        columns = pl.ds(pl.multiple_of((me_time ^ j) * width, width), width)
        x_high[:, columns] = high
        x_low[:, columns] = low
    if ramp:
        first = where_ref[3]
        receiver = first + lax.broadcasted_iota(jnp.int32, (rows, bins), 0)
        tapers = []
        for i in range(points):
            lowest, highest = lowest_ref[first_point + i], highest_ref[first_point + i]
            rising = jnp.clip((receiver - lowest + 1).astype(jnp.float32) / ramp, 0.0, 1.0)
            falling = jnp.clip((highest - receiver + 1).astype(jnp.float32) / ramp, 0.0, 1.0)
            tapers.append(obliquity_ref[first_point + i] * rising * falling)
    for k in range(parts):
        part = me_sp ^ k
        w_high, w_low = high_ref[part], low_ref[part]
        spectrum = (
            jnp.dot(x_high[...], w_high, preferred_element_type=jnp.float32)
            + jnp.dot(x_low[...], w_high, preferred_element_type=jnp.float32)
            + jnp.dot(x_high[...], w_low, preferred_element_type=jnp.float32)
        )
        for c in range(2):
            half = spectrum[:, c * bins : (c + 1) * bins].reshape(points, rows, bins)
            if ramp:
                for i in range(points):
                    out_refs[k][c, i] = half[i] * tapers[i]
            else:
                out_refs[k][c] = half


def transform(pieces, table, where, parts, ramp=0, taper=()):
    points, rows, width = pieces[0].shape
    samples, bins = table[0].shape[1], table[0].shape[2] // 2
    shape = (2, points, rows, bins)
    return pl.pallas_call(
        lambda *refs: transform_kernel(len(pieces), parts, ramp, *refs),
        out_shape=[jax.ShapeDtypeStruct(shape, jnp.float32)] * parts,
        in_specs=[SMEM] * (1 + len(taper)) + [VMEM] * (len(pieces) + 2),
        out_specs=[VMEM] * parts,
        scratch_shapes=[pltpu.VMEM((points * rows, samples), jnp.bfloat16)] * 2,
        compiler_params=pltpu.CompilerParams(vmem_limit_bytes=32 * 2**20),
        cost_estimate=pl.CostEstimate(
            flops=6 * points * rows * samples * bins * 2 * parts,
            bytes_accessed=8 * points * rows * samples + 8 * samples * bins * parts,
            transcendentals=0,
        ),
        name="transform",
    )(where, *taper, *pieces, *table)


GROUP = 2


def product_kernel(count, *refs):
    shot_refs, receiver_refs, out_ref = refs[:count], refs[count : 2 * count], refs[2 * count]
    _, shots, receivers, bins = out_ref.shape
    points = shot_refs[0].shape[1]

    def shot_group(g, _):
        def add_point(k, x, sums):
            r_re, r_im = receiver_refs[k][0, x], receiver_refs[k][1, x]
            r_sum = r_re + r_im
            new = []
            for i in range(GROUP):
                s_re = shot_refs[k][0, x, pl.ds(g * GROUP + i, 1), :]
                s_im = shot_refs[k][1, x, pl.ds(g * GROUP + i, 1), :]
                s_sum = s_re + s_im
                a, b, c = sums[3 * i : 3 * i + 3]
                new += [a + s_re * r_re, b + s_im * r_im, c + s_sum * r_sum]
            return tuple(new)

        sums = (jnp.zeros((receivers, bins), jnp.float32),) * (3 * GROUP)
        for k in range(count):
            sums = lax.fori_loop(0, points, lambda x, s, k=k: add_point(k, x, s), sums, unroll=2)
        for i in range(GROUP):
            a, b, c = sums[3 * i : 3 * i + 3]
            out_ref[0, g * GROUP + i] = a - b
            out_ref[1, g * GROUP + i] = c - a - b
        return 0

    lax.fori_loop(0, shots // GROUP, shot_group, 0)


def product(shot_blocks, receiver_blocks):
    count = len(shot_blocks)
    _, points, shots, bins = shot_blocks[0].shape
    receivers = receiver_blocks[0].shape[2]
    return pl.pallas_call(
        lambda *refs: product_kernel(count, *refs),
        out_shape=jax.ShapeDtypeStruct((2, shots, receivers, bins), jnp.float32),
        in_specs=[VMEM] * (2 * count),
        out_specs=VMEM,
        compiler_params=pltpu.CompilerParams(vmem_limit_bytes=32 * 2**20),
        cost_estimate=pl.CostEstimate(
            flops=8 * count * points * shots * receivers * bins,
            bytes_accessed=8 * (count * points * (shots + receivers) + shots * receivers) * bins,
            transcendentals=0,
        ),
        name="product",
    )(*shot_blocks, *receiver_blocks)


def exchange(block, axis, size, step):
    return lax.ppermute(block, axis, [(i, i ^ step) for i in range(size)])


def solution(mesh):
    n_src, n_rcv, n_sp = mesh.shape["src"], mesh.shape["rcv"], mesh.shape["sp"]

    def local(shot_traces, surface_receiver_traces, obliquity, lowest_receiver_index, hi_index):
        receivers = surface_receiver_traces.shape[1]
        samples = shot_traces.shape[2] * n_rcv
        table = tuple(jnp.asarray(t) for t in split_table(samples, NF, n_sp))
        me_src, me_rcv, me_sp = (lax.axis_index(a) for a in ("src", "rcv", "sp"))

        shot_pieces = [shot_traces] + [exchange(shot_traces, "rcv", n_rcv, j) for j in range(1, n_rcv)]
        receiver_pieces = [surface_receiver_traces] + [
            exchange(surface_receiver_traces, "src", n_src, j) for j in range(1, n_src)
        ]
        zero = jnp.int32(0)
        receiver_out = transform(
            receiver_pieces,
            table,
            jnp.stack([me_src, me_sp, zero, me_rcv * receivers]),
            n_sp,
            receivers * n_rcv // 8,
            (obliquity, lowest_receiver_index, hi_index),
        )
        receiver_blocks = [receiver_out[0]] + [
            exchange(receiver_out[k], "sp", n_sp, k) for k in range(1, n_sp)
        ]
        shot_out = transform(shot_pieces, table, jnp.stack([me_rcv, me_sp, zero, zero]), n_sp)
        shot_blocks = [shot_out[0]] + [exchange(shot_out[k], "sp", n_sp, k) for k in range(1, n_sp)]
        out = product(shot_blocks, receiver_blocks)
        return out.transpose(3, 0, 1, 2)

    placed = (P("sp", "src", "rcv"), P("sp", "rcv", "src"), P("sp"), P("sp"), P("sp"))
    return jax.shard_map(
        local, mesh=mesh, in_specs=placed, out_specs=P("sp", None, "src", "rcv"), check_vma=False
    )
```

```python
import math

import jax
import jax.numpy as jnp
import numpy as np
from jax import lax
from jax.experimental import pallas as pl
from jax.experimental.pallas import tpu as pltpu
from jax.sharding import PartitionSpec as P

NF = 512
VMEM = pl.BlockSpec(memory_space=pltpu.VMEM)
SMEM = pl.BlockSpec(memory_space=pltpu.SMEM)
ANY = pl.BlockSpec(memory_space=pl.ANY)
HBM = pl.BlockSpec(memory_space=pltpu.HBM)
COST = pl.CostEstimate(flops=1, bytes_accessed=1, transcendentals=0)
PARAMS = pltpu.CompilerParams(vmem_limit_bytes=16 * 2**20)


def cut_kernel(n_src, chunks, receiver_ref, shot_ref, *refs):
    receiver_outs, shot_outs, sems = refs[:n_src], refs[n_src : n_src + chunks], refs[-1]
    part = receiver_outs[0].shape[0]
    me = lax.axis_index("src")
    copies = []
    for j in range(n_src):
        span = pl.ds((me ^ j) * part, part)
        copies.append(pltpu.make_async_copy(receiver_ref.at[span], receiver_outs[j], sems.at[2 * j]))
        chunk, place = divmod(j * part, shot_outs[0].shape[0])
        copies.append(
            pltpu.make_async_copy(
                shot_ref.at[span], shot_outs[chunk].at[pl.ds(place, part)], sems.at[2 * j + 1]
            )
        )
    for copy in copies:
        copy.start()
    for copy in copies:
        copy.wait()


def cut(receiver_traces, shot_traces, n_src, chunks):
    points = receiver_traces.shape[0]
    out = pl.pallas_call(
        lambda *refs: cut_kernel(n_src, chunks, *refs),
        out_shape=[
            jax.ShapeDtypeStruct((points // n,) + a.shape[1:], a.dtype)
            for a, n in ((receiver_traces, n_src), (shot_traces, chunks))
            for _ in range(n)
        ],
        in_specs=[HBM, HBM],
        out_specs=[VMEM] * (n_src + chunks),
        scratch_shapes=[pltpu.SemaphoreType.DMA((2 * n_src,))],
        compiler_params=pltpu.CompilerParams(vmem_limit_bytes=60 * 2**20),
        cost_estimate=COST,
        name="cut",
    )(receiver_traces, shot_traces)
    return out[:n_src], out[n_src:]


def stage_kernel(coarse_ref, fine_ref, high_ref, low_ref):
    parts, steps, bins = fine_ref.shape[1:]

    def rows(a, _):
        for p in range(parts):
            cos_a, sin_a = coarse_ref[0, p, pl.ds(a, 1), :], coarse_ref[1, p, pl.ds(a, 1), :]
            cos_b, sin_b = fine_ref[0, p], fine_ref[1, p]
            span = pl.ds(pl.multiple_of(a * steps, steps), steps)
            both = jnp.concatenate([cos_a * cos_b - sin_a * sin_b, -(sin_a * cos_b + cos_a * sin_b)], axis=1)
            high = both.astype(jnp.bfloat16)
            high_ref[p, span, :] = high
            low_ref[p, span, :] = (both - high.astype(jnp.float32)).astype(jnp.bfloat16)
        return 0

    lax.fori_loop(0, coarse_ref.shape[2], rows, 0)


def fourier_table(samples, bins, parts):
    steps = 32

    def angles(times):
        freqs = np.arange(bins, dtype=np.int64)[None, :]
        phases = (times[:, None] * freqs % samples) * (2.0 * math.pi / samples)
        table = np.stack([np.cos(phases), np.sin(phases)]).astype(np.float32)
        return jnp.asarray(table.reshape(2, len(times), parts, bins // parts).transpose(0, 2, 1, 3))

    coarse = angles(np.arange(samples // steps, dtype=np.int64) * steps)
    fine = angles(np.arange(steps, dtype=np.int64))
    return pl.pallas_call(
        stage_kernel,
        out_shape=[jax.ShapeDtypeStruct((parts, samples, 2 * (bins // parts)), jnp.bfloat16)] * 2,
        in_specs=[VMEM] * 2,
        out_specs=[VMEM] * 2,
        compiler_params=PARAMS,
        cost_estimate=COST,
        name="fourier",
    )(coarse, fine)


def transform_kernel(pieces, parts, axis, ramp, *refs):
    if ramp:
        (obliquity_ref, lowest_ref, highest_ref), refs = refs[:3], refs[3:]
    piece_refs, refs = refs[:pieces], refs[pieces:]
    high_ref, low_ref = refs[:2]
    out_refs, (x_high, x_low) = refs[-2 - parts : -2], refs[-2:]
    points, rows, width = piece_refs[0].shape
    bins = out_refs[0].shape[-1]
    me_time, me_sp = lax.axis_index(axis), lax.axis_index("sp")
    for j in range(pieces):
        x = piece_refs[j][...].reshape(points * rows, width)
        high = x.astype(jnp.bfloat16)
        low = (x - high.astype(jnp.float32)).astype(jnp.bfloat16)
        columns = pl.ds(pl.multiple_of((me_time ^ j) * width, width), width)
        x_high[:, columns] = high
        x_low[:, columns] = low
    tapers = []
    if ramp:
        first = lax.axis_index("rcv") * rows
        receiver = first + lax.broadcasted_iota(jnp.int32, (rows, bins), 0)
        for i in range(points):
            point = lax.axis_index("src") * points + i
            lowest, highest = lowest_ref[point], highest_ref[point]
            rising = jnp.clip((receiver - lowest + 1).astype(jnp.float32) / ramp, 0.0, 1.0)
            falling = jnp.clip((highest - receiver + 1).astype(jnp.float32) / ramp, 0.0, 1.0)
            tapers.append(obliquity_ref[point] * rising * falling)
    for k in range(parts):
        part = me_sp ^ k
        w_high, w_low = high_ref[part], low_ref[part]
        spectrum = (
            jnp.dot(x_high[...], w_high, preferred_element_type=jnp.float32)
            + jnp.dot(x_low[...], w_high, preferred_element_type=jnp.float32)
            + jnp.dot(x_high[...], w_low, preferred_element_type=jnp.float32)
        )
        for c in range(2):
            half = spectrum[:, c * bins : (c + 1) * bins]
            if ramp:
                for i in range(points):
                    span = slice(i * rows, (i + 1) * rows)
                    out_refs[k][c, span] = half[span] * tapers[i]
            else:
                out_refs[k][c] = half


def transform(pieces, table, parts, axis, ramp=0, taper=(), after=()):
    points, rows, _ = pieces[0].shape
    samples, bins = table[0].shape[1], table[0].shape[2] // 2
    total = points * rows
    return pl.pallas_call(
        lambda *refs: transform_kernel(len(pieces), parts, axis, ramp, *refs),
        out_shape=[jax.ShapeDtypeStruct((2, total, bins), jnp.float32)] * parts,
        in_specs=[SMEM] * len(taper) + [VMEM] * (len(pieces) + 2) + [ANY] * len(after),
        out_specs=[VMEM] * parts,
        scratch_shapes=[pltpu.VMEM((total, samples), jnp.bfloat16)] * 2,
        compiler_params=PARAMS,
        cost_estimate=COST,
        name="transform",
    )(*taper, *pieces, *table, *after)


GROUP = 2


def product_kernel(terms, count, carried, rows, *refs):
    in_refs, total_refs, out_ref = refs[:count], refs[count : count + carried], refs[-1]
    shots, receivers = rows
    bins = out_ref.shape[-1]

    def shot_group(g, _):
        def add_point(term, x, sums):
            shot, shot_row, receiver, receiver_row, _ = term
            span = pl.ds(pl.multiple_of(receiver_row + x * receivers, 8), receivers)
            r_re, r_im = in_refs[receiver][0, span, :], in_refs[receiver][1, span, :]
            r_sum = r_re + r_im
            new = []
            for i in range(GROUP):
                line = pl.ds(shot_row + x * shots + g * GROUP + i, 1)
                s_re, s_im = in_refs[shot][0, line, :], in_refs[shot][1, line, :]
                s_sum = s_re + s_im
                a, b, c = sums[3 * i : 3 * i + 3]
                new += [a + s_re * r_re, b + s_im * r_im, c + s_sum * r_sum]
            return tuple(new)

        sums = (jnp.zeros((receivers, bins), jnp.float32),) * (3 * GROUP)
        for term in terms:
            step = lambda x, s, term=term: add_point(term, x, s)
            sums = lax.fori_loop(0, term[4], step, sums, unroll=2 if term[4] % 2 == 0 else 1)
        for i in range(GROUP):
            a, b, c = sums[3 * i : 3 * i + 3]
            real, imaginary = a - b, c - a - b
            if carried:
                real += total_refs[0][0, g * GROUP + i]
                imaginary += total_refs[0][1, g * GROUP + i]
            out_ref[0, g * GROUP + i] = real
            out_ref[1, g * GROUP + i] = imaginary
        return 0

    lax.fori_loop(0, shots // GROUP, shot_group, 0)


def product(terms, shots, receivers, total=None):
    blocks, described = [], []

    def place(block):
        for i, known in enumerate(blocks):
            if known is block:
                return i
        blocks.append(block)
        return len(blocks) - 1

    for shot, shot_row, receiver, receiver_row, points in terms:
        described.append((place(shot), shot_row, place(receiver), receiver_row, points))
    bins = blocks[0].shape[-1]
    carried = () if total is None else (total,)
    points = sum(term[4] for term in described)
    return pl.pallas_call(
        lambda *refs: product_kernel(described, len(blocks), len(carried), (shots, receivers), *refs),
        out_shape=jax.ShapeDtypeStruct((2, shots, receivers, bins), jnp.float32),
        in_specs=[VMEM] * (len(blocks) + len(carried)),
        out_specs=VMEM,
        compiler_params=PARAMS,
        cost_estimate=COST,
        name="product",
    )(*blocks, *carried)


def exchange(block, axis, size, step):
    return lax.ppermute(block, axis, [(i, i ^ step) for i in range(size)])


def gather(block, axis, size):
    pieces, step = {0: block}, size // 2
    while step:
        pieces |= {j ^ step: exchange(piece, axis, size, step) for j, piece in pieces.items()}
        step //= 2
    return [pieces[j] for j in range(size)]


def swap(blocks, axis, size):
    return [blocks[0]] + [exchange(blocks[step], axis, size, step) for step in range(1, size)]


def solution(mesh):
    n_src, n_rcv, n_sp = mesh.shape["src"], mesh.shape["rcv"], mesh.shape["sp"]

    def local(shot_traces, surface_receiver_traces, obliquity, lowest_receiver_index, hi_index):
        points, receivers = surface_receiver_traces.shape[:2]
        shots = shot_traces.shape[1]
        samples = shot_traces.shape[2] * n_rcv
        chunks, part = 2, points // n_src

        receiver_parts, shot_parts = cut(surface_receiver_traces, shot_traces, n_src, chunks)
        receiver_pieces = swap(receiver_parts, "src", n_src)
        shot_pieces = [gather(chunk, "rcv", n_rcv) for chunk in shot_parts]
        table = fourier_table(samples, NF, n_sp)

        near = n_sp // 2
        ramp = receivers * n_rcv // 8
        taper = (obliquity, lowest_receiver_index, hi_index)
        out = swap(transform(receiver_pieces, table, n_sp, "src", ramp, taper), "sp", n_sp)
        r = [gather(block, "src", n_src) for block in out]
        s = []
        for pieces in shot_pieces:
            out = swap(transform(pieces, table, n_sp, "rcv", after=(out[near],)), "sp", n_sp)
            s.append(out)

        def terms(chunk, k):
            held = n_src // chunks
            return [
                (s[chunk][k], j * part * shots, r[k][chunk * held + j], 0, part) for j in range(held)
            ]

        total = product(sum([terms(0, k) for k in range(n_sp)], []), shots, receivers)
        for span in (range(near), range(near, n_sp - 1), range(n_sp - 1, n_sp)):
            total = product(sum([terms(1, k) for k in span], []), shots, receivers, total)
        return total.transpose(3, 0, 1, 2)

    placed = (P("sp", "src", "rcv"), P("sp", "rcv", "src"), P("sp"), P("sp"), P("sp"))
    return jax.shard_map(
        local, mesh=mesh, in_specs=placed, out_specs=P("sp", None, "src", "rcv"), check_vma=False
    )
```

```python
import functools
import math

import jax
import jax.numpy as jnp
import numpy as np
from jax import lax
from jax.experimental import pallas as pl
from jax.experimental.pallas import tpu as pltpu
from jax.sharding import PartitionSpec as P

NF = 512
VMEM = pl.BlockSpec(memory_space=pltpu.VMEM)
SMEM = pl.BlockSpec(memory_space=pltpu.SMEM)
ANY = pl.BlockSpec(memory_space=pl.ANY)
HBM = pl.BlockSpec(memory_space=pltpu.HBM)
COST = pl.CostEstimate(flops=0, bytes_accessed=0, transcendentals=0)


def room(*arrays):
    need = 2**20
    for a in arrays:
        *lead, rows, columns = (1, 1, *a.shape)
        rows, columns = -(-rows // 16) * 16, -(-columns // 128) * 128
        need += math.prod(lead) * rows * columns * a.dtype.itemsize
    return pltpu.CompilerParams(vmem_limit_bytes=need)


def order(arrays, after):
    count = len(arrays)

    def kernel(*refs):
        del refs

    return pl.pallas_call(
        kernel,
        out_shape=[jax.ShapeDtypeStruct(a.shape, a.dtype) for a in arrays],
        in_specs=[ANY] * (count + len(after)),
        out_specs=[ANY] * count,
        input_output_aliases={i: i for i in range(count)},
        compiler_params=room(),
        cost_estimate=COST,
        name="order",
    )(*arrays, *after)


def tables_kernel(angles_ref, high_ref, low_ref):
    _, parts, _, bins = angles_ref.shape
    samples = high_ref.shape[1]
    coarse = samples // STEPS

    def table_rows(a, _):
        for p in range(parts):
            cos_a, sin_a = angles_ref[0, p, pl.ds(a, 1), :], angles_ref[1, p, pl.ds(a, 1), :]
            cos_b, sin_b = angles_ref[0, p, coarse:], angles_ref[1, p, coarse:]
            span = pl.ds(pl.multiple_of(a * STEPS, STEPS), STEPS)
            cosine = cos_a * cos_b - sin_a * sin_b
            both = jnp.concatenate([cosine, -(sin_a * cos_b + cos_a * sin_b)], axis=1)
            high = both.astype(jnp.bfloat16)
            high_ref[p, span, :] = high
            low_ref[p, span, :] = (both - high.astype(jnp.float32)).astype(jnp.bfloat16)
        return 0

    lax.fori_loop(0, coarse, table_rows, 0)


STEPS = 32


def tables(samples, bins, parts):
    times = np.concatenate([np.arange(samples // STEPS) * STEPS, np.arange(STEPS)]).astype(np.int64)
    freqs = np.arange(bins, dtype=np.int64)[None, :]
    phases = (times[:, None] * freqs % samples) * (2.0 * math.pi / samples)
    angles = np.stack([np.cos(phases), np.sin(phases)]).astype(np.float32)
    part = bins // parts
    angles = angles.reshape(2, len(times), parts, part).transpose(0, 2, 1, 3)
    angles = jnp.asarray(angles)
    out = [jax.ShapeDtypeStruct((parts, samples, 2 * part), jnp.bfloat16)] * 2
    return pl.pallas_call(
        tables_kernel,
        out_shape=out,
        in_specs=[VMEM],
        out_specs=[VMEM] * 2,
        compiler_params=room(angles, *out),
        cost_estimate=COST,
        name="tables",
    )(angles)


def tapers(obliquity, lowest, highest, first, rows, ramp, bins):
    receiver = first + lax.broadcasted_iota(jnp.int32, (lowest.shape[0], rows, bins), 1)
    lowest, highest = lowest[:, None, None], highest[:, None, None]
    rising = jnp.clip((receiver - lowest + 1).astype(jnp.float32) / ramp, 0.0, 1.0)
    falling = jnp.clip((highest - receiver + 1).astype(jnp.float32) / ramp, 0.0, 1.0)
    return obliquity[:, None, None] * rising * falling


def transform_kernel(steps, tapered, added, axis, chosen, points, spans, *refs):
    piece_refs, (high_ref, low_ref), refs = refs[: len(steps)], refs[len(steps) : len(steps) + 2], refs[len(steps) + 2 :]
    added_refs, (x_high, x_low) = refs[tapered : tapered + added], refs[-2:]
    pairs = high_ref.shape[0] // 2
    out_refs = refs[-2 - len(spans) : -2]
    _, rows, width = piece_refs[0].shape
    bins = out_refs[0].shape[-1]
    me_src, me_time, me_sp = (lax.axis_index(a) for a in ("src", axis, "sp"))

    def own(i):
        return pl.ds((me_src ^ chosen[i]) * points, points)

    for j, piece_ref in enumerate(piece_refs):
        for i in range(len(chosen)):
            span = slice(None) if piece_ref.shape[0] == points else own(i)
            x = piece_ref[span].reshape(points * rows, width)
            high = x.astype(jnp.bfloat16)
            low = (x - high.astype(jnp.float32)).astype(jnp.bfloat16)
            place = slice(i * points * rows, (i + 1) * points * rows)
            x_high[place, j * width : (j + 1) * width] = high
            x_low[place, j * width : (j + 1) * width] = low
    for k in range(2 * pairs):
        part = me_sp ^ k
        spectrum = 0.0
        for j, step in enumerate(steps):
            times = pl.ds(pl.multiple_of((me_time ^ step) * width, width), width)
            w_high, w_low = high_ref[part, times, :], low_ref[part, times, :]
            high, low = (x[:, j * width : (j + 1) * width] for x in (x_high, x_low))
            spectrum += (
                jnp.dot(high, w_high, preferred_element_type=jnp.float32)
                + jnp.dot(low, w_high, preferred_element_type=jnp.float32)
                + jnp.dot(high, w_low, preferred_element_type=jnp.float32)
            )
        for c in range(2):
            half = spectrum[:, c * bins : (c + 1) * bins]
            if tapered:
                half = half * refs[0][own(0)].reshape(points * rows, bins)
            for i, (q, first, count) in enumerate(spans):
                if q == k // 2:
                    value = half[first : first + count]
                    out_refs[i][k % 2, c] = value + added_refs[i][k % 2, c] if added else value


def transform(pieces, table, axis, chosen, points, cuts, taper=(), added=(), after=()):
    steps, pieces = tuple(pieces), list(pieces.values())
    rows, width = pieces[0].shape[1:]
    bins = table[0].shape[2] // 2
    total = points * len(chosen) * rows
    spans = [(q, i * (total // n), total // n) for q, n in enumerate(cuts) for i in range(n)]
    out = [jax.ShapeDtypeStruct((2, 2, count, bins), jnp.float32) for _, _, count in spans]
    split = [jax.ShapeDtypeStruct((total, len(steps) * width), jnp.bfloat16)] * 2
    spectrum = jax.ShapeDtypeStruct((total, 2 * bins), jnp.float32)
    return pl.pallas_call(
        lambda *refs: transform_kernel(steps, len(taper), len(added), axis, chosen, points, spans, *refs),
        out_shape=out,
        in_specs=[VMEM] * (len(pieces) + 2 + len(taper) + len(added)) + [ANY] * len(after),
        out_specs=[VMEM] * len(spans),
        scratch_shapes=[pltpu.VMEM(x.shape, x.dtype) for x in split],
        compiler_params=room(*pieces, *table, *taper, *added, *out, *split, *[spectrum] * 4),
        cost_estimate=COST,
        name="transform",
    )(*pieces, *table, *taper, *added, *after)


GROUP = 2


def product_kernel(terms, count, carried, rows, *refs):
    in_refs, total_refs, out_ref = refs[:count], refs[count : count + carried], refs[-1]
    shots, receivers = rows
    bins = out_ref.shape[-1]

    def shot_group(g, _):
        def add_point(term, x, sums):
            half, shot, shot_row, receiver, _ = term
            span = pl.ds(pl.multiple_of(x * receivers, 8), receivers)
            r_re, r_im = in_refs[receiver][half, 0, span, :], in_refs[receiver][half, 1, span, :]
            r_sum = r_re + r_im
            new = []
            for i in range(GROUP):
                line = pl.ds(shot_row + x * shots + g * GROUP + i, 1)
                s_re, s_im = in_refs[shot][half, 0, line, :], in_refs[shot][half, 1, line, :]
                s_sum = s_re + s_im
                a, b, c = sums[3 * i : 3 * i + 3]
                new += [a + s_re * r_re, b + s_im * r_im, c + s_sum * r_sum]
            return tuple(new)

        sums = (jnp.zeros((receivers, bins), jnp.float32),) * (3 * GROUP)
        for term in terms:
            step = lambda x, s, term=term: add_point(term, x, s)
            sums = lax.fori_loop(0, term[4], step, sums, unroll=2 if term[4] % 2 == 0 else 1)
        for i in range(GROUP):
            a, b, c = sums[3 * i : 3 * i + 3]
            real, imaginary = a - b, c - a - b
            if carried:
                real += total_refs[0][0, g * GROUP + i]
                imaginary += total_refs[0][1, g * GROUP + i]
            out_ref[0, g * GROUP + i] = real
            out_ref[1, g * GROUP + i] = imaginary
        return 0

    lax.fori_loop(0, shots // GROUP, shot_group, 0)


def product(terms, shots, receivers, total=None, after=()):
    blocks, described = [], []

    def place(block):
        for i, known in enumerate(blocks):
            if known is block:
                return i
        blocks.append(block)
        return len(blocks) - 1

    for half, shot, shot_row, receiver, points in terms:
        described.append((half, place(shot), shot_row, place(receiver), points))
    bins = blocks[0].shape[-1]
    carried = () if total is None else (total,)
    points = sum(term[4] for term in described)
    out = jax.ShapeDtypeStruct((2, shots, receivers, bins), jnp.float32)
    return pl.pallas_call(
        lambda *refs: product_kernel(described, len(blocks), len(carried), (shots, receivers), *refs),
        out_shape=out,
        in_specs=[VMEM] * (len(blocks) + len(carried)) + [ANY] * len(after),
        out_specs=VMEM,
        compiler_params=room(*blocks, *carried, out),
        cost_estimate=COST,
        name="product",
    )(*blocks, *carried, *after)


def exchange(block, axis, size, step):
    return lax.ppermute(block, axis, [(i, i ^ step) for i in range(size)])


def gather(block, axis, size, stop=1):
    pieces, step = {0: block}, size // 2
    while step >= stop:
        pieces |= {j ^ step: exchange(piece, axis, size, step) for j, piece in pieces.items()}
        step //= 2
    return [pieces[j] for j in range(0, size, stop)]


def solution(mesh):
    n_src, n_rcv, n_sp = mesh.shape["src"], mesh.shape["rcv"], mesh.shape["sp"]

    def local(shot_traces, surface_receiver_traces, obliquity, lowest_receiver_index, hi_index):
        points, receivers = surface_receiver_traces.shape[:2]
        shots = shot_traces.shape[1]
        samples = shot_traces.shape[2] * n_rcv
        part = points // n_src
        me = lax.axis_index("src")

        def own(array, j):
            return lax.dynamic_slice_in_dim(array, (me ^ j) * part, part)

        receiver_pieces = [own(surface_receiver_traces, 0)] + [
            exchange(own(surface_receiver_traces, j), "src", n_src, j) for j in range(1, n_src)
        ]
        table = tables(samples, NF, n_sp)
        taper = tapers(
            obliquity,
            lowest_receiver_index,
            hi_index,
            lax.axis_index("rcv") * receivers,
            receivers,
            receivers * n_rcv // 8,
            NF // n_sp,
        )

        def cross(blocks, count):
            return [
                block if i < 1 else exchange(block, "sp", n_sp, 2 * (1 + (i - 1) // count))
                for i, block in enumerate(blocks)
            ]

        def core(block):
            return exchange(block, "sp", n_sp, 1)

        def late(array, *after):
            return order([array], after)[0]

        chips = range(n_sp // 2)
        receiver_pieces = dict(enumerate(receiver_pieces))
        out = transform(receiver_pieces, table, "src", (0,), part, [1] * len(chips), (taper,))
        token, r_first = out[0], cross(out, 1)
        r_near = [gather(r_first[0], "src", n_src)]
        r_far = [[core(r_first[0])]]

        even = gather(shot_traces, "rcv", n_rcv, 2)
        beside = exchange(shot_traces, "rcv", n_rcv, 1)
        passed = order(even[1:], [token, beside])
        near = {0: shot_traces, 1: beside} | {2 * j: piece for j, piece in enumerate(passed, 1)}
        last = {2 * j + 1: exchange(piece, "rcv", n_rcv, 1) for j, piece in enumerate(passed, 1)}
        shot_transform = functools.partial(
            transform, axis="rcv", chosen=tuple(range(n_src)), points=part, cuts=[1] + [2] * (len(chips) - 1)
        )
        out = shot_transform(near, table)
        out = shot_transform(last, table, added=out, after=(r_first[-1], r_far[0][0]))
        token, s_near = out[0], cross(out, 2)
        s_far = [core(s_near[0])]
        for q in chips[1:]:
            r_near.append(gather(late(r_first[q], token), "src", n_src))
        r_far[0] += [core(late(block, token)) for block in r_near[0][1:]]

        held = n_src // 2

        def terms(chunk, pair, half):
            shot = (s_near, s_far)[half]
            block = shot[2 * pair - 1 + chunk] if pair else shot[0]
            first = 0 if pair else chunk * held
            return [
                (
                    half,
                    block,
                    (first + j) * part * shots,
                    (r_near, r_far)[half][pair][chunk * held + j],
                    part,
                )
                for j in range(held)
            ]

        pairs = chips[1:]
        first = [(0, 0, 0), (0, 0, 1), (1, 0, 0), (1, 0, 1)]
        total = product(sum([terms(*x) for x in first], []), shots, receivers)
        for q in pairs:
            s_near[2 * q - 1] = late(s_near[2 * q - 1], total)
        total = product(sum([terms(0, q, 0) for q in pairs], []), shots, receivers, total)
        for q in pairs:
            s_near[2 * q] = late(s_near[2 * q], total)
            s_far += [core(s_near[2 * q - 1]), core(s_near[2 * q])]
            r_far.append([core(late(block, total)) for block in r_near[q]])
        second = [(0, q, 1) for q in pairs] + [(1, q, 0) for q in pairs]
        after = [r_far[q][-1] for q in pairs]
        total = product(sum([terms(*x) for x in second], []), shots, receivers, total, after)
        total = product(sum([terms(1, q, 1) for q in pairs], []), shots, receivers, total)
        return total.transpose(3, 0, 1, 2)

    placed = (P("sp", "src", "rcv"), P("sp", "rcv", "src"), P("sp"), P("sp"), P("sp"))
    return jax.shard_map(
        local, mesh=mesh, in_specs=placed, out_specs=P("sp", None, "src", "rcv"), check_vma=False
    )
```

```python
import functools
import math

import jax
import jax.numpy as jnp
import numpy as np
from jax import lax
from jax.experimental import pallas as pl
from jax.experimental.pallas import tpu as pltpu
from jax.sharding import PartitionSpec as P

NF = 512
VMEM = pl.BlockSpec(memory_space=pltpu.VMEM)
SMEM = pl.BlockSpec(memory_space=pltpu.SMEM)
ANY = pl.BlockSpec(memory_space=pl.ANY)
HBM = pl.BlockSpec(memory_space=pltpu.HBM)
COST = pl.CostEstimate(flops=0, bytes_accessed=0, transcendentals=0)


def room(*arrays):
    need = 2**20
    for a in arrays:
        *lead, rows, columns = (1, 1, *a.shape)
        rows, columns = -(-rows // 16) * 16, -(-columns // 128) * 128
        need += math.prod(lead) * rows * columns * a.dtype.itemsize
    return pltpu.CompilerParams(vmem_limit_bytes=need)


def order(arrays, after):
    count = len(arrays)

    def kernel(*refs):
        del refs

    return pl.pallas_call(
        kernel,
        out_shape=[jax.ShapeDtypeStruct(a.shape, a.dtype) for a in arrays],
        in_specs=[ANY] * (count + len(after)),
        out_specs=[ANY] * count,
        input_output_aliases={i: i for i in range(count)},
        compiler_params=room(),
        cost_estimate=COST,
        name="order",
    )(*arrays, *after)


def tables_kernel(angles_ref, high_ref, low_ref):
    _, parts, _, bins = angles_ref.shape
    samples = high_ref.shape[1]
    coarse = samples // STEPS

    def table_rows(a, _):
        for p in range(parts):
            cos_a, sin_a = angles_ref[0, p, pl.ds(a, 1), :], angles_ref[1, p, pl.ds(a, 1), :]
            cos_b, sin_b = angles_ref[0, p, coarse:], angles_ref[1, p, coarse:]
            span = pl.ds(pl.multiple_of(a * STEPS, STEPS), STEPS)
            cosine = cos_a * cos_b - sin_a * sin_b
            both = jnp.concatenate([cosine, -(sin_a * cos_b + cos_a * sin_b)], axis=1)
            high = both.astype(jnp.bfloat16)
            high_ref[p, span, :] = high
            low_ref[p, span, :] = (both - high.astype(jnp.float32)).astype(jnp.bfloat16)
        return 0

    lax.fori_loop(0, coarse, table_rows, 0)


STEPS = 32


def tables(samples, bins, parts):
    times = np.concatenate([np.arange(samples // STEPS) * STEPS, np.arange(STEPS)]).astype(np.int64)
    freqs = np.arange(bins, dtype=np.int64)[None, :]
    phases = (times[:, None] * freqs % samples) * (2.0 * math.pi / samples)
    angles = np.stack([np.cos(phases), np.sin(phases)]).astype(np.float32)
    part = bins // parts
    angles = angles.reshape(2, len(times), parts, part).transpose(0, 2, 1, 3)
    angles = jnp.asarray(angles)
    out = [jax.ShapeDtypeStruct((parts, samples, 2 * part), jnp.bfloat16)] * 2
    return pl.pallas_call(
        tables_kernel,
        out_shape=out,
        in_specs=[VMEM],
        out_specs=[VMEM] * 2,
        compiler_params=room(angles, *out),
        cost_estimate=COST,
        name="tables",
    )(angles)


def tapers(obliquity, lowest, highest, first, rows, ramp, bins):
    receiver = first + lax.broadcasted_iota(jnp.int32, (lowest.shape[0], rows, bins), 1)
    lowest, highest = lowest[:, None, None], highest[:, None, None]
    rising = jnp.clip((receiver - lowest + 1).astype(jnp.float32) / ramp, 0.0, 1.0)
    falling = jnp.clip((highest - receiver + 1).astype(jnp.float32) / ramp, 0.0, 1.0)
    return obliquity[:, None, None] * rising * falling


def transform_kernel(steps, tapered, added, axis, chosen, points, spans, *refs):
    piece_refs, (high_ref, low_ref), refs = refs[: len(steps)], refs[len(steps) : len(steps) + 2], refs[len(steps) + 2 :]
    added_refs, (x_high, x_low) = refs[tapered : tapered + added], refs[-2:]
    pairs = high_ref.shape[0] // 2
    out_refs = refs[-2 - len(spans) : -2]
    _, rows, width = piece_refs[0].shape
    bins = out_refs[0].shape[-1]
    me_src, me_time, me_sp = (lax.axis_index(a) for a in ("src", axis, "sp"))

    def own(i):
        return pl.ds((me_src ^ chosen[i]) * points, points)

    for j, piece_ref in enumerate(piece_refs):
        for i in range(len(chosen)):
            span = slice(None) if piece_ref.shape[0] == points else own(i)
            x = piece_ref[span].reshape(points * rows, width)
            high = x.astype(jnp.bfloat16)
            low = (x - high.astype(jnp.float32)).astype(jnp.bfloat16)
            place = slice(i * points * rows, (i + 1) * points * rows)
            x_high[place, j * width : (j + 1) * width] = high
            x_low[place, j * width : (j + 1) * width] = low
    for k in range(2 * pairs):
        part = me_sp ^ k
        spectrum = 0.0
        for j, step in enumerate(steps):
            times = pl.ds(pl.multiple_of((me_time ^ step) * width, width), width)
            w_high, w_low = high_ref[part, times, :], low_ref[part, times, :]
            high, low = (x[:, j * width : (j + 1) * width] for x in (x_high, x_low))
            spectrum += (
                jnp.dot(high, w_high, preferred_element_type=jnp.float32)
                + jnp.dot(low, w_high, preferred_element_type=jnp.float32)
                + jnp.dot(high, w_low, preferred_element_type=jnp.float32)
            )
        for c in range(2):
            half = spectrum[:, c * bins : (c + 1) * bins]
            if tapered:
                half = half * refs[0][own(0)].reshape(points * rows, bins)
            for i, (q, first, count) in enumerate(spans):
                if q == k // 2:
                    value = half[first : first + count]
                    out_refs[i][k % 2, c] = value + added_refs[i][k % 2, c] if added else value


def transform(pieces, table, axis, chosen, points, cuts, taper=(), added=(), after=()):
    steps, pieces = tuple(pieces), list(pieces.values())
    rows, width = pieces[0].shape[1:]
    bins = table[0].shape[2] // 2
    total = points * len(chosen) * rows
    spans = []
    for q, cut in enumerate(cuts):
        edges = [0, *(point * rows for point in cut), total]
        spans += [(q, start, stop - start) for start, stop in zip(edges, edges[1:])]
    out = [jax.ShapeDtypeStruct((2, 2, count, bins), jnp.float32) for _, _, count in spans]
    split = [jax.ShapeDtypeStruct((total, len(steps) * width), jnp.bfloat16)] * 2
    spectrum = jax.ShapeDtypeStruct((total, 2 * bins), jnp.float32)
    return pl.pallas_call(
        lambda *refs: transform_kernel(steps, len(taper), len(added), axis, chosen, points, spans, *refs),
        out_shape=out,
        in_specs=[VMEM] * (len(pieces) + 2 + len(taper) + len(added)) + [ANY] * len(after),
        out_specs=[VMEM] * len(spans),
        scratch_shapes=[pltpu.VMEM(x.shape, x.dtype) for x in split],
        compiler_params=room(*pieces, *table, *taper, *added, *out, *split, *[spectrum] * 4),
        cost_estimate=COST,
        name="transform",
    )(*pieces, *table, *taper, *added, *after)


GROUP = 4


def product_kernel(terms, count, carried, rows, sends, *refs):
    in_refs, total_refs = refs[:count], refs[count : count + carried]
    shots, receivers = rows
    if sends:
        send_ref, out_ref, sems = refs[-3:]
    else:
        out_ref = refs[-1]
    bins = out_ref.shape[-1]

    def copy(g, c):
        span = pl.ds(g * GROUP, GROUP)
        return pltpu.make_async_copy(out_ref.at[c, span], send_ref.at[c, span], sems.at[g, c])

    for number, (half, shot, shot_row, receiver, receiver_row, points) in enumerate(terms):
        before = out_ref if number else total_refs[0] if carried else None

        def shot_group(g, _):
            sums = [jnp.zeros((receivers, bins), jnp.float32)] * (3 * GROUP)
            for x in range(points):
                span = slice(receiver_row + x * receivers, receiver_row + (x + 1) * receivers)
                r_re, r_im = in_refs[receiver][half, 0, span, :], in_refs[receiver][half, 1, span, :]
                r_sum = r_re + r_im
                for i in range(GROUP):
                    line = pl.ds(shot_row + x * shots + g * GROUP + i, 1)
                    s_re, s_im = in_refs[shot][half, 0, line, :], in_refs[shot][half, 1, line, :]
                    s_sum = s_re + s_im
                    sums[3 * i] += s_re * r_re
                    sums[3 * i + 1] += s_im * r_im
                    sums[3 * i + 2] += s_sum * r_sum
            for i in range(GROUP):
                a, b, c = sums[3 * i : 3 * i + 3]
                real, imaginary = a - b, c - a - b
                if before is not None:
                    real += before[0, g * GROUP + i]
                    imaginary += before[1, g * GROUP + i]
                out_ref[0, g * GROUP + i] = real
                out_ref[1, g * GROUP + i] = imaginary
            if sends and number == len(terms) - 1:
                copy(g, 0).start()
                copy(g, 1).start()
            return 0

        lax.fori_loop(0, shots // GROUP, shot_group, 0)
    if sends:

        def arrive(g, _):
            copy(g, 0).wait()
            copy(g, 1).wait()
            return 0

        lax.fori_loop(0, shots // GROUP, arrive, 0)


def product(terms, shots, receivers, total=None, after=(), last=False):
    blocks, described = [], []

    def place(block):
        for i, known in enumerate(blocks):
            if known is block:
                return i
        blocks.append(block)
        return len(blocks) - 1

    for half, shot, shot_row, receiver, receiver_row, points in terms:
        described.append((half, place(shot), shot_row, place(receiver), receiver_row, points))
    bins = blocks[0].shape[-1]
    carried = () if total is None else (total,)
    out = jax.ShapeDtypeStruct((2, shots, receivers, bins), jnp.float32)
    sends = [pltpu.VMEM(out.shape, out.dtype), pltpu.SemaphoreType.DMA((shots // GROUP, 2))]
    return pl.pallas_call(
        lambda *refs: product_kernel(described, len(blocks), len(carried), (shots, receivers), last, *refs),
        out_shape=out,
        in_specs=[VMEM] * (len(blocks) + len(carried)) + [ANY] * len(after),
        out_specs=HBM if last else VMEM,
        scratch_shapes=sends if last else [],
        compiler_params=room(*blocks, *carried, out),
        cost_estimate=COST,
        name="product",
    )(*blocks, *carried, *after)


def exchange(block, axis, size, step):
    return lax.ppermute(block, axis, [(i, i ^ step) for i in range(size)])


def gather(block, axis, size, stop=1):
    pieces, step = {0: block}, size // 2
    while step >= stop:
        pieces |= {j ^ step: exchange(piece, axis, size, step) for j, piece in pieces.items()}
        step //= 2
    return [pieces[j] for j in range(0, size, stop)]


def solution(mesh):
    n_src, n_rcv, n_sp = mesh.shape["src"], mesh.shape["rcv"], mesh.shape["sp"]

    def local(shot_traces, surface_receiver_traces, obliquity, lowest_receiver_index, hi_index):
        points, receivers = surface_receiver_traces.shape[:2]
        shots = shot_traces.shape[1]
        samples = shot_traces.shape[2] * n_rcv
        part = points // n_src
        me = lax.axis_index("src")

        def own(array, j):
            return lax.dynamic_slice_in_dim(array, (me ^ j) * part, part)

        receiver_pieces = [own(surface_receiver_traces, 0)] + [
            exchange(own(surface_receiver_traces, j), "src", n_src, j) for j in range(1, n_src)
        ]
        table = tables(samples, NF, n_sp)
        taper = tapers(
            obliquity,
            lowest_receiver_index,
            hi_index,
            lax.axis_index("rcv") * receivers,
            receivers,
            receivers * n_rcv // 8,
            NF // n_sp,
        )

        def cross(blocks, count):
            return [
                block if i < 1 else exchange(block, "sp", n_sp, 2 * (1 + (i - 1) // count))
                for i, block in enumerate(blocks)
            ]

        def core(block):
            return exchange(block, "sp", n_sp, 1)

        def late(array, *after):
            return order([array], after)[0]

        chips = range(n_sp // 2)
        receiver_pieces = dict(enumerate(receiver_pieces))
        out = transform(receiver_pieces, table, "src", (0,), part, [()] * len(chips), (taper,))
        token, r_first = out[0], cross(out, 1)
        r_near = [gather(r_first[0], "src", n_src)]
        r_far = [[core(r_first[0])]]

        cut = points - 3 * points // 8
        even = gather(shot_traces, "rcv", n_rcv, 2)
        beside = exchange(shot_traces, "rcv", n_rcv, 1)
        beside, *passed = order([beside, *even[1:]], [token])
        near = {0: shot_traces, 1: beside} | {2 * j: piece for j, piece in enumerate(passed, 1)}
        last = {2 * j + 1: exchange(piece, "rcv", n_rcv, 1) for j, piece in enumerate(passed, 1)}
        shot_transform = functools.partial(
            transform, axis="rcv", chosen=tuple(range(n_src)), points=part, cuts=[()] + [(cut,)] * (len(chips) - 1)
        )
        out = shot_transform(near, table)
        out = shot_transform(last, table, added=out, after=(r_first[-1], r_far[0][0]))
        token, s_near = out[0], cross(out, 2)
        s_far = [core(s_near[0])]
        for q in chips[1:]:
            r_near.append(gather(late(r_first[q], token), "src", n_src))
        r_far[0] += [core(late(block, token)) for block in r_near[0][1:]]

        def terms(chunk, pair, half):
            low, high = ((0, cut), (cut, points))[chunk]
            block = (s_near, s_far)[half][2 * pair - 1 + chunk if pair else 0]
            found = []
            for j in range(n_src):
                start, stop = max(low, j * part), min(high, (j + 1) * part)
                if start < stop:
                    shot_row = (start - (low if pair else 0)) * shots
                    receiver = (r_near, r_far)[half][pair][j]
                    found.append((half, block, shot_row, receiver, (start - j * part) * receivers, stop - start))
            return found

        pairs = chips[1:]
        first = [(0, 0, 0), (0, 0, 1), (1, 0, 0), (1, 0, 1)]
        total = product(sum([terms(*x) for x in first], []), shots, receivers)
        for q in pairs:
            s_near[2 * q - 1] = late(s_near[2 * q - 1], total)
        total = product(sum([terms(0, q, 0) for q in pairs], []), shots, receivers, total)
        for q in pairs:
            s_near[2 * q] = late(s_near[2 * q], total)
            s_far += [core(s_near[2 * q - 1]), core(s_near[2 * q])]
            r_far.append([core(block) for block in r_near[q]])
        second = [(0, q, 1) for q in pairs] + [(1, q, 0) for q in pairs]
        after = [r_far[q][-1] for q in pairs]
        total = product(sum([terms(*x) for x in second], []), shots, receivers, total, after)
        total = product(sum([terms(1, q, 1) for q in pairs], []), shots, receivers, total, last=True)
        return total.transpose(3, 0, 1, 2)

    placed = (P("sp", "src", "rcv"), P("sp", "rcv", "src"), P("sp"), P("sp"), P("sp"))
    return jax.shard_map(
        local, mesh=mesh, in_specs=placed, out_specs=P("sp", None, "src", "rcv"), check_vma=False
    )
```

```python
import functools
import math

import jax
import jax.numpy as jnp
import numpy as np
from jax import lax
from jax.experimental import pallas as pl
from jax.experimental.pallas import tpu as pltpu
from jax.sharding import PartitionSpec as P

NF = 512
VMEM = pl.BlockSpec(memory_space=pltpu.VMEM)
SMEM = pl.BlockSpec(memory_space=pltpu.SMEM)
ANY = pl.BlockSpec(memory_space=pl.ANY)
HBM = pl.BlockSpec(memory_space=pltpu.HBM)


def cost(flops=0):
    return pl.CostEstimate(flops=flops, bytes_accessed=0, transcendentals=0)


def room(*arrays):
    need = 2**20
    for a in arrays:
        *lead, rows, columns = (1, 1, *a.shape)
        rows, columns = -(-rows // 16) * 16, -(-columns // 128) * 128
        need += math.prod(lead) * rows * columns * a.dtype.itemsize
    return pltpu.CompilerParams(vmem_limit_bytes=need)


def order(arrays, after, flops=0):
    count = len(arrays)

    def kernel(*refs):
        del refs

    return pl.pallas_call(
        kernel,
        out_shape=[jax.ShapeDtypeStruct(a.shape, a.dtype) for a in arrays],
        in_specs=[ANY] * (count + len(after)),
        out_specs=[ANY] * count,
        input_output_aliases={i: i for i in range(count)},
        compiler_params=room(),
        cost_estimate=cost(flops),
        name="order",
    )(*arrays, *after)


def runs(low, high, part):
    found = []
    for j in range(low // part, -(-high // part)):
        start, stop = max(low, j * part), min(high, (j + 1) * part)
        found.append((j, start - j * part, stop - start, start - low))
    return found


def pick(array, edges, part, after, flops=0):
    bounds = list(zip(edges, edges[1:]))
    out = [jax.ShapeDtypeStruct((high - low,) + array.shape[1:], array.dtype) for low, high in bounds]

    def kernel(array_ref, *refs):
        me = lax.axis_index("src")
        for (low, high), out_ref in zip(bounds, refs[len(after) :]):
            for j, first, count, place in runs(low, high, part):
                out_ref[place : place + count] = array_ref[pl.ds((me ^ j) * part + first, count)]

    return pl.pallas_call(
        kernel,
        out_shape=out,
        in_specs=[VMEM] + [ANY] * len(after),
        out_specs=[VMEM] * len(out),
        compiler_params=room(array, *out),
        cost_estimate=cost(flops),
        name="pick",
    )(array, *after)


def tables_kernel(angles_ref, high_ref, low_ref):
    _, parts, _, bins = angles_ref.shape
    samples = high_ref.shape[1]
    coarse = samples // STEPS

    def table_rows(a, _):
        for p in range(parts):
            cos_a, sin_a = angles_ref[0, p, pl.ds(a, 1), :], angles_ref[1, p, pl.ds(a, 1), :]
            cos_b, sin_b = angles_ref[0, p, coarse:], angles_ref[1, p, coarse:]
            span = pl.ds(pl.multiple_of(a * STEPS, STEPS), STEPS)
            cosine = cos_a * cos_b - sin_a * sin_b
            both = jnp.concatenate([cosine, -(sin_a * cos_b + cos_a * sin_b)], axis=1)
            high = both.astype(jnp.bfloat16)
            high_ref[p, span, :] = high
            low_ref[p, span, :] = (both - high.astype(jnp.float32)).astype(jnp.bfloat16)
        return 0

    lax.fori_loop(0, coarse, table_rows, 0)


STEPS = 32


def tables(samples, bins, parts):
    times = np.concatenate([np.arange(samples // STEPS) * STEPS, np.arange(STEPS)]).astype(np.int64)
    freqs = np.arange(bins, dtype=np.int64)[None, :]
    phases = (times[:, None] * freqs % samples) * (2.0 * math.pi / samples)
    angles = np.stack([np.cos(phases), np.sin(phases)]).astype(np.float32)
    part = bins // parts
    angles = angles.reshape(2, len(times), parts, part).transpose(0, 2, 1, 3)
    angles = jnp.asarray(angles)
    out = [jax.ShapeDtypeStruct((parts, samples, 2 * part), jnp.bfloat16)] * 2
    return pl.pallas_call(
        tables_kernel,
        out_shape=out,
        in_specs=[VMEM],
        out_specs=[VMEM] * 2,
        compiler_params=room(angles, *out),
        cost_estimate=cost(),
        name="tables",
    )(angles)


def tapers(obliquity, lowest, highest, first, rows, ramp, bins):
    receiver = first + lax.broadcasted_iota(jnp.int32, (lowest.shape[0], rows, bins), 1)
    lowest, highest = lowest[:, None, None], highest[:, None, None]
    rising = jnp.clip((receiver - lowest + 1).astype(jnp.float32) / ramp, 0.0, 1.0)
    falling = jnp.clip((highest - receiver + 1).astype(jnp.float32) / ramp, 0.0, 1.0)
    return obliquity[:, None, None] * rising * falling


def transform_kernel(steps, tapered, added, axis, low, high, part, points, spans, *refs):
    piece_refs, (high_ref, low_ref), refs = refs[: len(steps)], refs[len(steps) : len(steps) + 2], refs[len(steps) + 2 :]
    added_refs, (x_high, x_low) = refs[tapered : tapered + added], refs[-2:]
    pairs = high_ref.shape[0] // 2
    out_refs = refs[-2 - len(spans) : -2]
    _, rows, width = piece_refs[0].shape
    bins = out_refs[0].shape[-1]
    me_src, me_time, me_sp = (lax.axis_index(a) for a in ("src", axis, "sp"))

    for j, piece_ref in enumerate(piece_refs):
        for i, first, count, place in runs(low, high, part):
            whole = piece_ref.shape[0] == points
            x = piece_ref[pl.ds((me_src ^ i) * part + first, count) if whole else slice(place, place + count)]
            x = x.reshape(count * rows, width)
            high_part = x.astype(jnp.bfloat16)
            low_part = (x - high_part.astype(jnp.float32)).astype(jnp.bfloat16)
            place = slice(place * rows, (place + count) * rows)
            x_high[place, j * width : (j + 1) * width] = high_part
            x_low[place, j * width : (j + 1) * width] = low_part
    for k in range(2 * pairs):
        device = me_sp ^ k
        spectrum = 0.0
        for j, step in enumerate(steps):
            times = pl.ds(pl.multiple_of((me_time ^ step) * width, width), width)
            w_high, w_low = high_ref[device, times, :], low_ref[device, times, :]
            x_hi, x_lo = (x[:, j * width : (j + 1) * width] for x in (x_high, x_low))
            spectrum += (
                jnp.dot(x_hi, w_high, preferred_element_type=jnp.float32)
                + jnp.dot(x_lo, w_high, preferred_element_type=jnp.float32)
                + jnp.dot(x_hi, w_low, preferred_element_type=jnp.float32)
            )
        for c in range(2):
            half = spectrum[:, c * bins : (c + 1) * bins]
            if tapered:
                own = pl.ds(me_src * part, part)
                half = half * refs[0][own].reshape(part * rows, bins)
            for i, (q, first, count) in enumerate(spans):
                if q == k // 2:
                    value = half[first : first + count]
                    out_refs[i][k % 2, c] = value + added_refs[i][k % 2, c] if added else value


def transform(pieces, table, axis, low, high, part, points, cuts, taper=(), added=(), after=(), flops=0):
    steps, pieces = tuple(pieces), list(pieces.values())
    rows, width = pieces[0].shape[1:]
    bins = table[0].shape[2] // 2
    total = (high - low) * rows
    spans = []
    for q, cut in enumerate(cuts):
        edges = [0, *((point - low) * rows for point in cut), total]
        spans += [(q, start, stop - start) for start, stop in zip(edges, edges[1:])]
    out = [jax.ShapeDtypeStruct((2, 2, count, bins), jnp.float32) for _, _, count in spans]
    split = [jax.ShapeDtypeStruct((total, len(steps) * width), jnp.bfloat16)] * 2
    spectrum = jax.ShapeDtypeStruct((total, 2 * bins), jnp.float32)
    return pl.pallas_call(
        lambda *refs: transform_kernel(steps, len(taper), len(added), axis, low, high, part, points, spans, *refs),
        out_shape=out,
        in_specs=[VMEM] * (len(pieces) + 2 + len(taper) + len(added)) + [ANY] * len(after),
        out_specs=[VMEM] * len(spans),
        scratch_shapes=[pltpu.VMEM(x.shape, x.dtype) for x in split],
        compiler_params=room(*pieces, *table, *taper, *added, *out, *split, *[spectrum] * 4),
        cost_estimate=cost(flops),
        name="transform",
    )(*pieces, *table, *taper, *added, *after)


GROUP = 4


def product_kernel(terms, count, carried, rows, sends, *refs):
    in_refs, total_refs = refs[:count], refs[count : count + carried]
    shots, receivers = rows
    if sends:
        send_ref, out_ref, sems = refs[-3:]
    else:
        out_ref = refs[-1]
    bins = out_ref.shape[-1]

    def copy(g, c):
        span = pl.ds(g * GROUP, GROUP)
        return pltpu.make_async_copy(out_ref.at[c, span], send_ref.at[c, span], sems.at[g, c])

    for number, (half, shot, shot_row, receiver, receiver_row, points) in enumerate(terms):
        before = out_ref if number else total_refs[0] if carried else None

        def shot_group(g, _):
            sums = [jnp.zeros((receivers, bins), jnp.float32)] * (3 * GROUP)
            for x in range(points):
                span = slice(receiver_row + x * receivers, receiver_row + (x + 1) * receivers)
                r_re, r_im = in_refs[receiver][half, 0, span, :], in_refs[receiver][half, 1, span, :]
                r_sum = r_re + r_im
                for i in range(GROUP):
                    line = pl.ds(shot_row + x * shots + g * GROUP + i, 1)
                    s_re, s_im = in_refs[shot][half, 0, line, :], in_refs[shot][half, 1, line, :]
                    s_sum = s_re + s_im
                    sums[3 * i] += s_re * r_re
                    sums[3 * i + 1] += s_im * r_im
                    sums[3 * i + 2] += s_sum * r_sum
            for i in range(GROUP):
                a, b, c = sums[3 * i : 3 * i + 3]
                real, imaginary = a - b, c - a - b
                if before is not None:
                    real += before[0, g * GROUP + i]
                    imaginary += before[1, g * GROUP + i]
                out_ref[0, g * GROUP + i] = real
                out_ref[1, g * GROUP + i] = imaginary
            if sends and number == len(terms) - 1:
                copy(g, 0).start()
                copy(g, 1).start()
            return 0

        lax.fori_loop(0, shots // GROUP, shot_group, 0)
    if sends:

        def arrive(g, _):
            copy(g, 0).wait()
            copy(g, 1).wait()
            return 0

        lax.fori_loop(0, shots // GROUP, arrive, 0)


def product(terms, shots, receivers, total=None, after=(), last=False):
    blocks, described = [], []

    def place(block):
        for i, known in enumerate(blocks):
            if known is block:
                return i
        blocks.append(block)
        return len(blocks) - 1

    for half, shot, shot_row, receiver, receiver_row, points in terms:
        described.append((half, place(shot), shot_row, place(receiver), receiver_row, points))
    bins = blocks[0].shape[-1]
    carried = () if total is None else (total,)
    out = jax.ShapeDtypeStruct((2, shots, receivers, bins), jnp.float32)
    sends = [pltpu.VMEM(out.shape, out.dtype), pltpu.SemaphoreType.DMA((shots // GROUP, 2))]
    return pl.pallas_call(
        lambda *refs: product_kernel(described, len(blocks), len(carried), (shots, receivers), last, *refs),
        out_shape=out,
        in_specs=[VMEM] * (len(blocks) + len(carried)) + [ANY] * len(after),
        out_specs=HBM if last else VMEM,
        scratch_shapes=sends if last else [],
        compiler_params=room(*blocks, *carried, out),
        cost_estimate=cost(),
        name="product",
    )(*blocks, *carried, *after)


def exchange(block, axis, size, step):
    return lax.ppermute(block, axis, [(i, i ^ step) for i in range(size)])


def gather(block, axis, size, stop=1):
    pieces, step = {0: block}, size // 2
    while step >= stop:
        pieces |= {j ^ step: exchange(piece, axis, size, step) for j, piece in pieces.items()}
        step //= 2
    return [pieces[j] for j in range(0, size, stop)]


def solution(mesh):
    n_src, n_rcv, n_sp = mesh.shape["src"], mesh.shape["rcv"], mesh.shape["sp"]

    def local(shot_traces, surface_receiver_traces, obliquity, lowest_receiver_index, hi_index):
        points, receivers = surface_receiver_traces.shape[:2]
        shots = shot_traces.shape[1]
        samples = shot_traces.shape[2] * n_rcv
        part = points // n_src
        me = lax.axis_index("src")

        def own(array, j):
            return lax.dynamic_slice_in_dim(array, (me ^ j) * part, part)

        receiver_pieces = [own(surface_receiver_traces, 0)] + [
            exchange(own(surface_receiver_traces, j), "src", n_src, j) for j in range(1, n_src)
        ]
        table = tables(samples, NF, n_sp)
        taper = tapers(
            obliquity,
            lowest_receiver_index,
            hi_index,
            lax.axis_index("rcv") * receivers,
            receivers,
            receivers * n_rcv // 8,
            NF // n_sp,
        )

        def cross(blocks, count):
            return [
                block if i < 1 else exchange(block, "sp", n_sp, 2 * (1 + (i - 1) // count))
                for i, block in enumerate(blocks)
            ]

        def core(block):
            return exchange(block, "sp", n_sp, 1)

        def late(array, *after):
            return order([array], after)[0]

        chips = range(n_sp // 2)
        receiver_pieces = dict(enumerate(receiver_pieces))
        out = transform(receiver_pieces, table, "src", 0, part, part, points, [()] * len(chips), (taper,))
        token, r_first = out[0], cross(out, 1)
        r_near = [gather(r_first[0], "src", n_src)]
        r_far = [[core(r_first[0])]]

        cut = points - 3 * points // 8
        even = gather(shot_traces, "rcv", n_rcv, 2)
        beside = exchange(shot_traces, "rcv", n_rcv, 1)
        beside = late(beside, token)
        edges = (0, cut, points)
        shot_transform = functools.partial(transform, table=table, axis="rcv", part=part, points=points)
        near = {0: shot_traces, 1: beside} | {2 * j: piece for j, piece in enumerate(even[1:], 1)}
        first = [pick(piece, edges[:2], part, [token, beside], 3 * 10**9) for piece in even[1:]]
        out = shot_transform(
            near, low=0, high=points, cuts=[(cut,)] * len(chips), after=[p[0] for p in first], flops=10**9
        )
        passed = [p + pick(piece, edges[1:], part, [out[0]]) for p, piece in zip(first, even[1:])]
        s_near = [None] * (2 * len(chips))
        after = r_far[0] + r_first[1:]
        for chunk, flops in ((0, 2500 * 10**6), (1, 8 * 10**9)):
            last = {2 * j + 1: exchange(p[chunk], "rcv", n_rcv, 1) for j, p in enumerate(passed, 1)}
            blocks = shot_transform(
                last,
                low=edges[chunk],
                high=edges[chunk + 1],
                cuts=[()] * len(chips),
                added=out[chunk::2],
                after=after,
                flops=flops,
            )
            s_near[chunk::2] = cross(blocks, 1)
            after, token = [blocks[0]], blocks[0]
        s_far = [core(s_near[0]), None]
        for q in chips[1:]:
            r_near.append(gather(late(r_first[q], token), "src", n_src))
        r_far[0] += [core(late(block, s_near[0])) for block in r_near[0][1:]]

        def terms(chunk, pair, half):
            block = (s_near, s_far)[half][2 * pair + chunk]
            return [
                (half, block, place * shots, (r_near, r_far)[half][pair][j], first * receivers, count)
                for j, first, count, place in runs(edges[chunk], edges[chunk + 1], part)
            ]

        pairs = chips[1:]
        first = [(0, 0, 0), (0, 0, 1), (1, 0, 0)]
        total = product(sum([terms(*x) for x in first], []), shots, receivers)
        for q in pairs:
            s_near[2 * q] = late(s_near[2 * q], total)
        s_far[1] = core(s_near[1])
        total = product(sum([terms(0, q, 0) for q in pairs] + [terms(1, 0, 1)], []), shots, receivers, total)
        for q in pairs:
            s_near[2 * q + 1] = late(s_near[2 * q + 1], total)
            s_far += [core(s_near[2 * q]), core(s_near[2 * q + 1])]
            r_far.append([core(block) for block in r_near[q]])
        second = [(0, q, 1) for q in pairs] + [(1, q, 0) for q in pairs]
        after = [r_far[q][-1] for q in pairs]
        total = product(sum([terms(*x) for x in second], []), shots, receivers, total, after)
        total = product(sum([terms(1, q, 1) for q in pairs], []), shots, receivers, total, last=True)
        return total.transpose(3, 0, 1, 2)

    placed = (P("sp", "src", "rcv"), P("sp", "rcv", "src"), P("sp"), P("sp"), P("sp"))
    return jax.shard_map(
        local, mesh=mesh, in_specs=placed, out_specs=P("sp", None, "src", "rcv"), check_vma=False
    )
```

```python
import functools
import math

import jax
import jax.numpy as jnp
import numpy as np
from jax import lax
from jax.experimental import pallas as pl
from jax.experimental.pallas import tpu as pltpu
from jax.sharding import PartitionSpec as P

NF = 512
VMEM = pl.BlockSpec(memory_space=pltpu.VMEM)
SMEM = pl.BlockSpec(memory_space=pltpu.SMEM)
ANY = pl.BlockSpec(memory_space=pl.ANY)
HBM = pl.BlockSpec(memory_space=pltpu.HBM)


def cost(flops=0):
    return pl.CostEstimate(flops=flops, bytes_accessed=0, transcendentals=0)


def room(*arrays):
    need = 2**20
    for a in arrays:
        *lead, rows, columns = (1, 1, *a.shape)
        rows, columns = -(-rows // 16) * 16, -(-columns // 128) * 128
        need += math.prod(lead) * rows * columns * a.dtype.itemsize
    return pltpu.CompilerParams(vmem_limit_bytes=need)


def order(arrays, after, flops=0):
    count = len(arrays)

    def kernel(*refs):
        del refs

    return pl.pallas_call(
        kernel,
        out_shape=[jax.ShapeDtypeStruct(a.shape, a.dtype) for a in arrays],
        in_specs=[ANY] * (count + len(after)),
        out_specs=[ANY] * count,
        input_output_aliases={i: i for i in range(count)},
        compiler_params=room(),
        cost_estimate=cost(flops),
        name="order",
    )(*arrays, *after)


def runs(low, high, part):
    found = []
    for j in range(low // part, -(-high // part)):
        start, stop = max(low, j * part), min(high, (j + 1) * part)
        found.append((j, start - j * part, stop - start, start - low))
    return found


def pick(array, edges, part, after, flops=0):
    bounds = list(zip(edges, edges[1:]))
    out = [jax.ShapeDtypeStruct((high - low,) + array.shape[1:], array.dtype) for low, high in bounds]

    def kernel(array_ref, *refs):
        me = lax.axis_index("src")
        for (low, high), out_ref in zip(bounds, refs[len(after) :]):
            for j, first, count, place in runs(low, high, part):
                out_ref[place : place + count] = array_ref[pl.ds((me ^ j) * part + first, count)]

    return pl.pallas_call(
        kernel,
        out_shape=out,
        in_specs=[VMEM] + [ANY] * len(after),
        out_specs=[VMEM] * len(out),
        compiler_params=room(array, *out),
        cost_estimate=cost(flops),
        name="pick",
    )(array, *after)


def tables_kernel(angles_ref, high_ref, low_ref):
    _, parts, _, bins = angles_ref.shape
    samples = high_ref.shape[1]
    coarse = samples // STEPS

    def table_rows(a, _):
        for p in range(parts):
            cos_a, sin_a = angles_ref[0, p, pl.ds(a, 1), :], angles_ref[1, p, pl.ds(a, 1), :]
            cos_b, sin_b = angles_ref[0, p, coarse:], angles_ref[1, p, coarse:]
            span = pl.ds(pl.multiple_of(a * STEPS, STEPS), STEPS)
            cosine = cos_a * cos_b - sin_a * sin_b
            both = jnp.concatenate([cosine, -(sin_a * cos_b + cos_a * sin_b)], axis=1)
            high = both.astype(jnp.bfloat16)
            high_ref[p, span, :] = high
            low_ref[p, span, :] = (both - high.astype(jnp.float32)).astype(jnp.bfloat16)
        return 0

    lax.fori_loop(0, coarse, table_rows, 0)


STEPS = 32


def tables(samples, bins, parts):
    times = np.concatenate([np.arange(samples // STEPS) * STEPS, np.arange(STEPS)]).astype(np.int64)
    freqs = np.arange(bins, dtype=np.int64)[None, :]
    phases = (times[:, None] * freqs % samples) * (2.0 * math.pi / samples)
    angles = np.stack([np.cos(phases), np.sin(phases)]).astype(np.float32)
    part = bins // parts
    angles = angles.reshape(2, len(times), parts, part).transpose(0, 2, 1, 3)
    angles = jnp.asarray(angles)
    out = [jax.ShapeDtypeStruct((parts, samples, 2 * part), jnp.bfloat16)] * 2
    return pl.pallas_call(
        tables_kernel,
        out_shape=out,
        in_specs=[VMEM],
        out_specs=[VMEM] * 2,
        compiler_params=room(angles, *out),
        cost_estimate=cost(),
        name="tables",
    )(angles)


def tapers(obliquity, lowest, highest, first, rows, ramp, bins):
    receiver = first + lax.broadcasted_iota(jnp.int32, (lowest.shape[0], rows, bins), 1)
    lowest, highest = lowest[:, None, None], highest[:, None, None]
    rising = jnp.clip((receiver - lowest + 1).astype(jnp.float32) / ramp, 0.0, 1.0)
    falling = jnp.clip((highest - receiver + 1).astype(jnp.float32) / ramp, 0.0, 1.0)
    return obliquity[:, None, None] * rising * falling


def transform_kernel(steps, tapered, added, axis, low, high, part, points, spans, *refs):
    piece_refs, (high_ref, low_ref), refs = refs[: len(steps)], refs[len(steps) : len(steps) + 2], refs[len(steps) + 2 :]
    added_refs, (x_high, x_low) = refs[tapered : tapered + added], refs[-2:]
    pairs = high_ref.shape[0] // 2
    out_refs = refs[-2 - len(spans) : -2]
    _, rows, width = piece_refs[0].shape
    bins = out_refs[0].shape[-1]
    me_src, me_time, me_sp = (lax.axis_index(a) for a in ("src", axis, "sp"))

    for j, piece_ref in enumerate(piece_refs):
        for i, first, count, place in runs(low, high, part):
            whole = piece_ref.shape[0] == points
            x = piece_ref[pl.ds((me_src ^ i) * part + first, count) if whole else slice(place, place + count)]
            x = x.reshape(count * rows, width)
            high_part = x.astype(jnp.bfloat16)
            low_part = (x - high_part.astype(jnp.float32)).astype(jnp.bfloat16)
            place = slice(place * rows, (place + count) * rows)
            x_high[place, j * width : (j + 1) * width] = high_part
            x_low[place, j * width : (j + 1) * width] = low_part
    for k in range(2 * pairs):
        device = me_sp ^ k
        spectrum = 0.0
        for j, step in enumerate(steps):
            times = pl.ds(pl.multiple_of((me_time ^ step) * width, width), width)
            w_high, w_low = high_ref[device, times, :], low_ref[device, times, :]
            x_hi, x_lo = (x[:, j * width : (j + 1) * width] for x in (x_high, x_low))
            spectrum += (
                jnp.dot(x_hi, w_high, preferred_element_type=jnp.float32)
                + jnp.dot(x_lo, w_high, preferred_element_type=jnp.float32)
                + jnp.dot(x_hi, w_low, preferred_element_type=jnp.float32)
            )
        for c in range(2):
            half = spectrum[:, c * bins : (c + 1) * bins]
            if tapered:
                own = pl.ds(me_src * part, part)
                half = half * refs[0][own].reshape(part * rows, bins)
            for i, (q, first, count) in enumerate(spans):
                if q == k // 2:
                    value = half[first : first + count]
                    out_refs[i][k % 2, c] = value + added_refs[i][k % 2, c] if added else value


def transform(pieces, table, axis, low, high, part, points, cuts, taper=(), added=(), after=(), flops=0):
    steps, pieces = tuple(pieces), list(pieces.values())
    rows, width = pieces[0].shape[1:]
    bins = table[0].shape[2] // 2
    total = (high - low) * rows
    spans = []
    for q, cut in enumerate(cuts):
        edges = [0, *((point - low) * rows for point in cut), total]
        spans += [(q, start, stop - start) for start, stop in zip(edges, edges[1:])]
    out = [jax.ShapeDtypeStruct((2, 2, count, bins), jnp.float32) for _, _, count in spans]
    split = [jax.ShapeDtypeStruct((total, len(steps) * width), jnp.bfloat16)] * 2
    spectrum = jax.ShapeDtypeStruct((total, 2 * bins), jnp.float32)
    return pl.pallas_call(
        lambda *refs: transform_kernel(steps, len(taper), len(added), axis, low, high, part, points, spans, *refs),
        out_shape=out,
        in_specs=[VMEM] * (len(pieces) + 2 + len(taper) + len(added)) + [ANY] * len(after),
        out_specs=[VMEM] * len(spans),
        scratch_shapes=[pltpu.VMEM(x.shape, x.dtype) for x in split],
        compiler_params=room(*pieces, *table, *taper, *added, *out, *split, *[spectrum] * 4),
        cost_estimate=cost(flops),
        name="transform",
    )(*pieces, *table, *taper, *added, *after)


GROUP = 4


def product_kernel(terms, count, carried, rows, sends, *refs):
    in_refs, total_refs = refs[:count], refs[count : count + carried]
    shots, receivers = rows
    if sends:
        send_ref, out_ref, sems = refs[-3:]
    else:
        out_ref = refs[-1]
    bins = out_ref.shape[-1]

    def copy(g, c):
        span = pl.ds(g * GROUP, GROUP)
        return pltpu.make_async_copy(out_ref.at[c, span], send_ref.at[c, span], sems.at[g, c])

    for number, (half, shot, shot_row, receiver, receiver_row, points) in enumerate(terms):
        before = out_ref if number else total_refs[0] if carried else None

        def shot_group(g, _):
            sums = [jnp.zeros((receivers, bins), jnp.float32)] * (3 * GROUP)
            for x in range(points):
                span = slice(receiver_row + x * receivers, receiver_row + (x + 1) * receivers)
                r_re, r_im = in_refs[receiver][half, 0, span, :], in_refs[receiver][half, 1, span, :]
                r_sum = r_re + r_im
                for i in range(GROUP):
                    line = pl.ds(shot_row + x * shots + g * GROUP + i, 1)
                    s_re, s_im = in_refs[shot][half, 0, line, :], in_refs[shot][half, 1, line, :]
                    s_sum = s_re + s_im
                    sums[3 * i] += s_re * r_re
                    sums[3 * i + 1] += s_im * r_im
                    sums[3 * i + 2] += s_sum * r_sum
            for i in range(GROUP):
                a, b, c = sums[3 * i : 3 * i + 3]
                real, imaginary = a - b, c - a - b
                if before is not None:
                    real += before[0, g * GROUP + i]
                    imaginary += before[1, g * GROUP + i]
                out_ref[0, g * GROUP + i] = real
                out_ref[1, g * GROUP + i] = imaginary
            if sends and number == len(terms) - 1:
                copy(g, 0).start()
                copy(g, 1).start()
            return 0

        lax.fori_loop(0, shots // GROUP, shot_group, 0)
    if sends:

        def arrive(g, _):
            copy(g, 0).wait()
            copy(g, 1).wait()
            return 0

        lax.fori_loop(0, shots // GROUP, arrive, 0)


def product(terms, shots, receivers, total=None, after=(), last=False):
    blocks, described = [], []

    def place(block):
        for i, known in enumerate(blocks):
            if known is block:
                return i
        blocks.append(block)
        return len(blocks) - 1

    for half, shot, shot_row, receiver, receiver_row, points in terms:
        described.append((half, place(shot), shot_row, place(receiver), receiver_row, points))
    bins = blocks[0].shape[-1]
    carried = () if total is None else (total,)
    out = jax.ShapeDtypeStruct((2, shots, receivers, bins), jnp.float32)
    sends = [pltpu.VMEM(out.shape, out.dtype), pltpu.SemaphoreType.DMA((shots // GROUP, 2))]
    return pl.pallas_call(
        lambda *refs: product_kernel(described, len(blocks), len(carried), (shots, receivers), last, *refs),
        out_shape=out,
        in_specs=[VMEM] * (len(blocks) + len(carried)) + [ANY] * len(after),
        out_specs=HBM if last else VMEM,
        scratch_shapes=sends if last else [],
        compiler_params=room(*blocks, *carried, out),
        cost_estimate=cost(),
        name="product",
    )(*blocks, *carried, *after)


def exchange(block, axis, size, step):
    return lax.ppermute(block, axis, [(i, i ^ step) for i in range(size)])


def gather(block, axis, size, stop=1):
    pieces, step = {0: block}, size // 2
    while step >= stop:
        pieces |= {j ^ step: exchange(piece, axis, size, step) for j, piece in pieces.items()}
        step //= 2
    return [pieces[j] for j in range(0, size, stop)]


def solution(mesh):
    n_src, n_rcv, n_sp = mesh.shape["src"], mesh.shape["rcv"], mesh.shape["sp"]

    def local(shot_traces, surface_receiver_traces, obliquity, lowest_receiver_index, hi_index):
        points, receivers = surface_receiver_traces.shape[:2]
        shots = shot_traces.shape[1]
        samples = shot_traces.shape[2] * n_rcv
        part = points // n_src
        me = lax.axis_index("src")

        def own(array, j):
            return lax.dynamic_slice_in_dim(array, (me ^ j) * part, part)

        receiver_pieces = [own(surface_receiver_traces, 0)] + [
            exchange(own(surface_receiver_traces, j), "src", n_src, j) for j in range(1, n_src)
        ]
        table = tables(samples, NF, n_sp)
        taper = tapers(
            obliquity,
            lowest_receiver_index,
            hi_index,
            lax.axis_index("rcv") * receivers,
            receivers,
            receivers * n_rcv // 8,
            NF // n_sp,
        )

        def cross(blocks, count):
            return [
                block if i < 1 else exchange(block, "sp", n_sp, 2 * (1 + (i - 1) // count))
                for i, block in enumerate(blocks)
            ]

        def core(block):
            return exchange(block, "sp", n_sp, 1)

        def late(array, *after):
            return order([array], after)[0]

        chips = range(n_sp // 2)
        receiver_pieces = dict(enumerate(receiver_pieces))
        out = transform(receiver_pieces, table, "src", 0, part, part, points, [()] * len(chips), (taper,))
        token, r_first = out[0], cross(out, 1)
        r_near = [gather(r_first[0], "src", n_src)]
        r_far = [[core(r_first[0])]]

        cut = points - 3 * points // 8
        even = gather(shot_traces, "rcv", n_rcv, 2)
        beside = exchange(shot_traces, "rcv", n_rcv, 1)
        edges = (0, cut, points)
        shot_transform = functools.partial(transform, table=table, axis="rcv", part=part, points=points)
        near = {0: shot_traces, 1: beside} | {2 * j: piece for j, piece in enumerate(even[1:], 1)}
        first = [pick(piece, edges[:2], part, [token], 3 * 10**9) for piece in even[1:]]
        out = shot_transform(
            near, low=0, high=points, cuts=[(cut,)] * len(chips), after=[p[0] for p in first], flops=10**9
        )
        passed = [p + pick(piece, edges[1:], part, [out[0]]) for p, piece in zip(first, even[1:])]
        s_near = [None] * (2 * len(chips))
        after = r_far[0] + r_first[1:]
        for chunk, flops in ((0, 2500 * 10**6), (1, 8 * 10**9)):
            last = {2 * j + 1: exchange(p[chunk], "rcv", n_rcv, 1) for j, p in enumerate(passed, 1)}
            blocks = shot_transform(
                last,
                low=edges[chunk],
                high=edges[chunk + 1],
                cuts=[()] * len(chips),
                added=out[chunk::2],
                after=after,
                flops=flops,
            )
            s_near[chunk::2] = cross(blocks, 1)
            after, token = [blocks[0]], blocks[0]
        s_far = [core(s_near[0]), None]
        for q in chips[1:]:
            r_near.append(gather(late(r_first[q], token), "src", n_src))
        r_far[0] += [core(late(block, s_near[0])) for block in r_near[0][1:]]

        def terms(chunk, pair, half):
            block = (s_near, s_far)[half][2 * pair + chunk]
            return [
                (half, block, place * shots, (r_near, r_far)[half][pair][j], first * receivers, count)
                for j, first, count, place in runs(edges[chunk], edges[chunk + 1], part)
            ]

        pairs = chips[1:]
        first = [(0, 0, 0), (0, 0, 1), (1, 0, 0)]
        total = product(sum([terms(*x) for x in first], []), shots, receivers)
        for q in pairs:
            s_near[2 * q] = late(s_near[2 * q], total)
        s_far[1] = core(s_near[1])
        total = product(sum([terms(0, q, 0) for q in pairs] + [terms(1, 0, 1)], []), shots, receivers, total)
        for q in pairs:
            s_near[2 * q + 1] = late(s_near[2 * q + 1], total)
            s_far += [core(s_near[2 * q]), core(s_near[2 * q + 1])]
            r_far.append([core(block) for block in r_near[q]])
        second = [(0, q, 1) for q in pairs] + [(1, q, 0) for q in pairs]
        after = [r_far[q][-1] for q in pairs]
        total = product(sum([terms(*x) for x in second], []), shots, receivers, total, after)
        total = product(sum([terms(1, q, 1) for q in pairs], []), shots, receivers, total, last=True)
        return total.transpose(3, 0, 1, 2)

    placed = (P("sp", "src", "rcv"), P("sp", "rcv", "src"), P("sp"), P("sp"), P("sp"))
    return jax.shard_map(
        local, mesh=mesh, in_specs=placed, out_specs=P("sp", None, "src", "rcv"), check_vma=False
    )
```

```python
import functools
import math

import jax
import jax.numpy as jnp
import numpy as np
from jax import lax
from jax.experimental import pallas as pl
from jax.experimental.pallas import tpu as pltpu
from jax.sharding import PartitionSpec as P

NF = 512
VMEM = pl.BlockSpec(memory_space=pltpu.VMEM)
SMEM = pl.BlockSpec(memory_space=pltpu.SMEM)
ANY = pl.BlockSpec(memory_space=pl.ANY)
HBM = pl.BlockSpec(memory_space=pltpu.HBM)


def cost(flops=0):
    return pl.CostEstimate(flops=flops, bytes_accessed=0, transcendentals=0)


def room(*arrays):
    need = 2**20
    for a in arrays:
        *lead, rows, columns = (1, 1, *a.shape)
        rows, columns = -(-rows // 16) * 16, -(-columns // 128) * 128
        need += math.prod(lead) * rows * columns * a.dtype.itemsize
    return pltpu.CompilerParams(vmem_limit_bytes=need)


def order(arrays, after, flops=0):
    count = len(arrays)

    def kernel(*refs):
        del refs

    return pl.pallas_call(
        kernel,
        out_shape=[jax.ShapeDtypeStruct(a.shape, a.dtype) for a in arrays],
        in_specs=[ANY] * (count + len(after)),
        out_specs=[ANY] * count,
        input_output_aliases={i: i for i in range(count)},
        compiler_params=room(),
        cost_estimate=cost(flops),
        name="order",
    )(*arrays, *after)


def runs(low, high, part):
    found = []
    for j in range(low // part, -(-high // part)):
        start, stop = max(low, j * part), min(high, (j + 1) * part)
        found.append((j, start - j * part, stop - start, start - low))
    return found


def pick(array, edges, part, after, flops=0):
    bounds = list(zip(edges, edges[1:]))
    out = [jax.ShapeDtypeStruct((high - low,) + array.shape[1:], array.dtype) for low, high in bounds]

    def kernel(array_ref, *refs):
        me = lax.axis_index("src")
        for (low, high), out_ref in zip(bounds, refs[len(after) :]):
            for j, first, count, place in runs(low, high, part):
                out_ref[place : place + count] = array_ref[pl.ds((me ^ j) * part + first, count)]

    return pl.pallas_call(
        kernel,
        out_shape=out,
        in_specs=[VMEM] + [ANY] * len(after),
        out_specs=[VMEM] * len(out),
        compiler_params=room(array, *out),
        cost_estimate=cost(flops),
        name="pick",
    )(array, *after)


def far_half(block):
    out = jax.ShapeDtypeStruct((1,) + block.shape[1:], block.dtype)

    def kernel(block_ref, out_ref):
        out_ref[0] = block_ref[1]

    return pl.pallas_call(
        kernel,
        out_shape=out,
        in_specs=[VMEM],
        out_specs=VMEM,
        compiler_params=room(block, out),
        cost_estimate=cost(),
        name="far_half",
    )(block)


def tables_kernel(angles_ref, high_ref, low_ref):
    _, parts, _, bins = angles_ref.shape
    samples = high_ref.shape[1]
    coarse = samples // STEPS

    def table_rows(a, _):
        for p in range(parts):
            cos_a, sin_a = angles_ref[0, p, pl.ds(a, 1), :], angles_ref[1, p, pl.ds(a, 1), :]
            cos_b, sin_b = angles_ref[0, p, coarse:], angles_ref[1, p, coarse:]
            span = pl.ds(pl.multiple_of(a * STEPS, STEPS), STEPS)
            cosine = cos_a * cos_b - sin_a * sin_b
            both = jnp.concatenate([cosine, -(sin_a * cos_b + cos_a * sin_b)], axis=1)
            high = both.astype(jnp.bfloat16)
            high_ref[p, span, :] = high
            low_ref[p, span, :] = (both - high.astype(jnp.float32)).astype(jnp.bfloat16)
        return 0

    lax.fori_loop(0, coarse, table_rows, 0)


STEPS = 32


def tables(samples, bins, parts):
    times = np.concatenate([np.arange(samples // STEPS) * STEPS, np.arange(STEPS)]).astype(np.int64)
    freqs = np.arange(bins, dtype=np.int64)[None, :]
    phases = (times[:, None] * freqs % samples) * (2.0 * math.pi / samples)
    angles = np.stack([np.cos(phases), np.sin(phases)]).astype(np.float32)
    part = bins // parts
    angles = angles.reshape(2, len(times), parts, part).transpose(0, 2, 1, 3)
    angles = jnp.asarray(angles)
    out = [jax.ShapeDtypeStruct((parts, samples, 2 * part), jnp.bfloat16)] * 2
    return pl.pallas_call(
        tables_kernel,
        out_shape=out,
        in_specs=[VMEM],
        out_specs=[VMEM] * 2,
        compiler_params=room(angles, *out),
        cost_estimate=cost(),
        name="tables",
    )(angles)


def tapers(obliquity, lowest, highest, first, rows, ramp, bins):
    receiver = first + lax.broadcasted_iota(jnp.int32, (lowest.shape[0], rows, bins), 1)
    lowest, highest = lowest[:, None, None], highest[:, None, None]
    rising = jnp.clip((receiver - lowest + 1).astype(jnp.float32) / ramp, 0.0, 1.0)
    falling = jnp.clip((highest - receiver + 1).astype(jnp.float32) / ramp, 0.0, 1.0)
    return obliquity[:, None, None] * rising * falling


def transform_kernel(steps, tapered, added, axis, low, high, part, points, spans, *refs):
    piece_refs, (high_ref, low_ref), refs = refs[: len(steps)], refs[len(steps) : len(steps) + 2], refs[len(steps) + 2 :]
    added_refs, (x_high, x_low) = refs[tapered : tapered + added], refs[-2:]
    pairs = high_ref.shape[0] // 2
    out_refs = refs[-2 - len(spans) : -2]
    _, rows, width = piece_refs[0].shape
    bins = out_refs[0].shape[-1]
    me_src, me_time, me_sp = (lax.axis_index(a) for a in ("src", axis, "sp"))

    for j, piece_ref in enumerate(piece_refs):
        for i, first, count, place in runs(low, high, part):
            whole = piece_ref.shape[0] == points
            x = piece_ref[pl.ds((me_src ^ i) * part + first, count) if whole else slice(place, place + count)]
            x = x.reshape(count * rows, width)
            high_part = x.astype(jnp.bfloat16)
            low_part = (x - high_part.astype(jnp.float32)).astype(jnp.bfloat16)
            place = slice(place * rows, (place + count) * rows)
            x_high[place, j * width : (j + 1) * width] = high_part
            x_low[place, j * width : (j + 1) * width] = low_part
    for k in range(2 * pairs):
        device = me_sp ^ k
        spectrum = 0.0
        for j, step in enumerate(steps):
            times = pl.ds(pl.multiple_of((me_time ^ step) * width, width), width)
            w_high, w_low = high_ref[device, times, :], low_ref[device, times, :]
            x_hi, x_lo = (x[:, j * width : (j + 1) * width] for x in (x_high, x_low))
            spectrum += (
                jnp.dot(x_hi, w_high, preferred_element_type=jnp.float32)
                + jnp.dot(x_lo, w_high, preferred_element_type=jnp.float32)
                + jnp.dot(x_hi, w_low, preferred_element_type=jnp.float32)
            )
        for c in range(2):
            half = spectrum[:, c * bins : (c + 1) * bins]
            if tapered:
                own = pl.ds(me_src * part, part)
                half = half * refs[0][own].reshape(part * rows, bins)
            for i, (q, first, count) in enumerate(spans):
                if q == k // 2:
                    value = half[first : first + count]
                    out_refs[i][k % 2, c] = value + added_refs[i][k % 2, c] if added else value


def transform(pieces, table, axis, low, high, part, points, cuts, taper=(), added=(), after=(), flops=0):
    steps, pieces = tuple(pieces), list(pieces.values())
    rows, width = pieces[0].shape[1:]
    bins = table[0].shape[2] // 2
    total = (high - low) * rows
    spans = []
    for q, cut in enumerate(cuts):
        edges = [0, *((point - low) * rows for point in cut), total]
        spans += [(q, start, stop - start) for start, stop in zip(edges, edges[1:])]
    out = [jax.ShapeDtypeStruct((2, 2, count, bins), jnp.float32) for _, _, count in spans]
    split = [jax.ShapeDtypeStruct((total, len(steps) * width), jnp.bfloat16)] * 2
    spectrum = jax.ShapeDtypeStruct((total, 2 * bins), jnp.float32)
    return pl.pallas_call(
        lambda *refs: transform_kernel(steps, len(taper), len(added), axis, low, high, part, points, spans, *refs),
        out_shape=out,
        in_specs=[VMEM] * (len(pieces) + 2 + len(taper) + len(added)) + [ANY] * len(after),
        out_specs=[VMEM] * len(spans),
        scratch_shapes=[pltpu.VMEM(x.shape, x.dtype) for x in split],
        compiler_params=room(*pieces, *table, *taper, *added, *out, *split, *[spectrum] * 4),
        cost_estimate=cost(flops),
        name="transform",
    )(*pieces, *table, *taper, *added, *after)


GROUP = 4


def product_kernel(terms, count, carried, rows, sends, *refs):
    in_refs, total_refs = refs[:count], refs[count : count + carried]
    shots, receivers = rows
    if sends:
        send_ref, out_ref, sems = refs[-3:]
    else:
        out_ref = refs[-1]
    bins = out_ref.shape[-1]

    def copy(g, c):
        span = pl.ds(g * GROUP, GROUP)
        return pltpu.make_async_copy(out_ref.at[c, span], send_ref.at[c, span], sems.at[g, c])

    for number, (half, shot, shot_row, receiver, receiver_row, points) in enumerate(terms):
        shot_half = min(half, in_refs[shot].shape[0] - 1)
        receiver_half = min(half, in_refs[receiver].shape[0] - 1)
        before = out_ref if number else total_refs[0] if carried else None

        def shot_group(g, _):
            sums = [jnp.zeros((receivers, bins), jnp.float32)] * (3 * GROUP)
            for x in range(points):
                span = slice(receiver_row + x * receivers, receiver_row + (x + 1) * receivers)
                r_re, r_im = in_refs[receiver][receiver_half, 0, span, :], in_refs[receiver][receiver_half, 1, span, :]
                r_sum = r_re + r_im
                for i in range(GROUP):
                    line = pl.ds(shot_row + x * shots + g * GROUP + i, 1)
                    s_re, s_im = in_refs[shot][shot_half, 0, line, :], in_refs[shot][shot_half, 1, line, :]
                    s_sum = s_re + s_im
                    sums[3 * i] += s_re * r_re
                    sums[3 * i + 1] += s_im * r_im
                    sums[3 * i + 2] += s_sum * r_sum
            for i in range(GROUP):
                a, b, c = sums[3 * i : 3 * i + 3]
                real, imaginary = a - b, c - a - b
                if before is not None:
                    real += before[0, g * GROUP + i]
                    imaginary += before[1, g * GROUP + i]
                out_ref[0, g * GROUP + i] = real
                out_ref[1, g * GROUP + i] = imaginary
            if sends and number == len(terms) - 1:
                copy(g, 0).start()
                copy(g, 1).start()
            return 0

        lax.fori_loop(0, shots // GROUP, shot_group, 0)
    if sends:

        def arrive(g, _):
            copy(g, 0).wait()
            copy(g, 1).wait()
            return 0

        lax.fori_loop(0, shots // GROUP, arrive, 0)


def product(terms, shots, receivers, total=None, after=(), last=False):
    blocks, described = [], []

    def place(block):
        for i, known in enumerate(blocks):
            if known is block:
                return i
        blocks.append(block)
        return len(blocks) - 1

    for half, shot, shot_row, receiver, receiver_row, points in terms:
        described.append((half, place(shot), shot_row, place(receiver), receiver_row, points))
    bins = blocks[0].shape[-1]
    carried = () if total is None else (total,)
    out = jax.ShapeDtypeStruct((2, shots, receivers, bins), jnp.float32)
    sends = [pltpu.VMEM(out.shape, out.dtype), pltpu.SemaphoreType.DMA((shots // GROUP, 2))]
    return pl.pallas_call(
        lambda *refs: product_kernel(described, len(blocks), len(carried), (shots, receivers), last, *refs),
        out_shape=out,
        in_specs=[VMEM] * (len(blocks) + len(carried)) + [ANY] * len(after),
        out_specs=HBM if last else VMEM,
        scratch_shapes=sends if last else [],
        compiler_params=room(*blocks, *carried, out),
        cost_estimate=cost(),
        name="product",
    )(*blocks, *carried, *after)


def exchange(block, axis, size, step):
    return lax.ppermute(block, axis, [(i, i ^ step) for i in range(size)])


def gather(block, axis, size, stop=1):
    pieces, step = {0: block}, size // 2
    while step >= stop:
        pieces |= {j ^ step: exchange(piece, axis, size, step) for j, piece in pieces.items()}
        step //= 2
    return [pieces[j] for j in range(0, size, stop)]


def solution(mesh):
    n_src, n_rcv, n_sp = mesh.shape["src"], mesh.shape["rcv"], mesh.shape["sp"]

    def local(shot_traces, surface_receiver_traces, obliquity, lowest_receiver_index, hi_index):
        points, receivers = surface_receiver_traces.shape[:2]
        shots = shot_traces.shape[1]
        samples = shot_traces.shape[2] * n_rcv
        part = points // n_src
        me = lax.axis_index("src")

        def own(array, j):
            return lax.dynamic_slice_in_dim(array, (me ^ j) * part, part)

        receiver_pieces = [own(surface_receiver_traces, 0)] + [
            exchange(own(surface_receiver_traces, j), "src", n_src, j) for j in range(1, n_src)
        ]
        table = tables(samples, NF, n_sp)
        taper = tapers(
            obliquity,
            lowest_receiver_index,
            hi_index,
            lax.axis_index("rcv") * receivers,
            receivers,
            receivers * n_rcv // 8,
            NF // n_sp,
        )

        def cross(blocks, count):
            return [
                block if i < 1 else exchange(block, "sp", n_sp, 2 * (1 + (i - 1) // count))
                for i, block in enumerate(blocks)
            ]

        def core(block):
            return exchange(block, "sp", n_sp, 1)

        def late(array, *after):
            return order([array], after)[0]

        chips = range(n_sp // 2)
        receiver_pieces = dict(enumerate(receiver_pieces))
        out = transform(receiver_pieces, table, "src", 0, part, part, points, [()] * len(chips), (taper,))
        token, r_first = out[0], cross(out, 1)
        r_near = [gather(r_first[0], "src", n_src)]
        r_far = [[core(r_first[0])]]

        cut = points - 3 * points // 8
        even = gather(shot_traces, "rcv", n_rcv, 2)
        beside = exchange(shot_traces, "rcv", n_rcv, 1)
        edges = (0, cut, points)
        shot_transform = functools.partial(transform, table=table, axis="rcv", part=part, points=points)
        near = {0: shot_traces, 1: beside} | {2 * j: piece for j, piece in enumerate(even[1:], 1)}
        first = [pick(piece, edges[:2], part, [token], 3 * 10**9) for piece in even[1:]]
        out = shot_transform(
            near, low=0, high=points, cuts=[(cut,)] * len(chips), after=[p[0] for p in first], flops=10**9
        )
        passed = [p + pick(piece, edges[1:], part, [out[0]]) for p, piece in zip(first, even[1:])]
        s_near = [None] * (2 * len(chips))
        after = r_far[0] + r_first[1:]
        for chunk, flops in ((0, 2500 * 10**6), (1, 8 * 10**9)):
            last = {2 * j + 1: exchange(p[chunk], "rcv", n_rcv, 1) for j, p in enumerate(passed, 1)}
            blocks = shot_transform(
                last,
                low=edges[chunk],
                high=edges[chunk + 1],
                cuts=[()] * len(chips),
                added=out[chunk::2],
                after=after,
                flops=flops,
            )
            s_near[chunk::2] = cross(blocks, 1)
            after, token = [blocks[0]], blocks[0]
        s_far = [core(s_near[0]), None]
        for q in chips[1:]:
            r_near.append(gather(late(r_first[q], token), "src", n_src))
        r_far[0] += [core(late(block, s_near[0])) for block in r_near[0][1:]]

        def terms(chunk, pair, half):
            block = (s_near, s_far)[half][2 * pair + chunk]
            return [
                (half, block, place * shots, (r_near, r_far)[half][pair][j], first * receivers, count)
                for j, first, count, place in runs(edges[chunk], edges[chunk + 1], part)
            ]

        pairs = chips[1:]
        s_far[1] = core(s_near[1])
        total = product(sum([terms(*x) for x in [(0, 0, 0), (0, 0, 1), (1, 0, 0), (1, 0, 1)]], []), shots, receivers)
        for q in pairs:
            s_near[2 * q] = late(s_near[2 * q], total)
        total = product(sum([terms(*x) for x in [(0, q, 0) for q in pairs]], []), shots, receivers, total)
        for q in pairs:
            s_far += [core(far_half(s_near[2 * q])), None]
            r_far.append([core(far_half(block)) for block in r_near[q]])
        total = product(sum([terms(0, q, 1) for q in pairs], []), shots, receivers, total)
        for q in pairs:
            s_near[2 * q + 1] = late(s_near[2 * q + 1], total)
            s_far[2 * q + 1] = core(far_half(s_near[2 * q + 1]))
        total = product(sum([terms(1, q, 0) for q in pairs], []), shots, receivers, total)
        total = product(sum([terms(1, q, 1) for q in pairs], []), shots, receivers, total, last=True)
        return total.transpose(3, 0, 1, 2)

    placed = (P("sp", "src", "rcv"), P("sp", "rcv", "src"), P("sp"), P("sp"), P("sp"))
    return jax.shard_map(
        local, mesh=mesh, in_specs=placed, out_specs=P("sp", None, "src", "rcv"), check_vma=False
    )
```
